256 devices in a mesh: dp: 32 (over y, z), tensor: 8 (over x, core).
Axes of the slice: x: 4, y: 4, z: 8, core: 2. Of those that a mesh axis runs over, the one named last changes fastest.
Arguments:
- new_states: bfloat16 [8192, 4, 5120], P(('dp', 'tensor')), may hold values from -6 to 6
- w_query: bfloat16 [5120, 4096], P(None, 'tensor'), may hold values from -0.078125 to 0.078125
- keyvalue_weight: bfloat16 [5120, 16, 128], P(None, 'tensor'), may hold values from -0.078125 to 0.078125
- keyvalue_pages: bfloat16 [1024, 16, 128, 128], P('dp', 'tensor'), may hold values from -110 to 110
- page_table: int32 [32, 32], P('dp'), may hold values from 0 to 31, each once within a row
- prompt_pages: int32 [32, 8], P('dp'), may hold values from 1 to 4, as said below
- share_prompt: int32 [32, 32], P('dp'), may hold values from 0 to 7, never falling along the last dimension, each value on 1 to 8 neighbouring positions
- share_group: int32 [32, 32], P('dp'), may hold values from 0 to 31, each once within a row
Outputs:
- attended: bfloat16 [8192, 4, 4096], P('dp', None, 'tensor')
The draws below stay inside these ranges and needn't reach their ends.
Inputs may be any that keep to these rules, and one draw needn't show every extreme that they name: `share_prompt`: each owner's shares of one prompt are consecutive, from 1 to 8 shares a prompt, so that a prompt has 8 to 64 samples; every prompt has a share. `share_group`: each row names every group once: every group decodes exactly one share of every owner. `page_table`: each row is a permutation of the owner's pages. `prompt_pages`: some prompt has exactly 4 pages and some exactly one.
All inputs are finite; a program needn't handle non-finite values.
Results may differ from the reference program's by a relative error of at most 0.012.
The reference program's roundings to bfloat16 on the way count: a program that leaves them out, or rounds other values in their place, can miss the bound.
Values may be sent and summed in bfloat16 or wider, within the bound.
No kernel may reach another device: no remote copies, remote signals or barrier semaphores. Data moves between devices by JAX's collectives and lax.ppermute only.
A program may use at most 192 MiB of HBM per device.

```python
import math
import jax
import jax.numpy as jnp
import numpy as np
from jax import lax

MODEL_WIDTH = 5120
QUERY_HEADS = 32
KEY_HEADS = 8
HEAD_SIZE = 128
PAGE_TOKENS = 128
LONGEST_PAGES = 4
DECODE_STEPS = 4
PROMPT_SAMPLES = 8
PR_DEV = 8
OWNER_PAGES = 32
GROUP_SAMPLES = 256
ROWS = 8192
N_DP = 32


def draw_keyvalue_pages(key, part):
    key = jax.random.fold_in(key, 7)
    first = jax.random.fold_in(key, 0)
    fourth_item = jax.random.fold_in(key, 3)
    array_shape = (N_DP * OWNER_PAGES, KEY_HEADS, 2, PAGE_TOKENS, HEAD_SIZE)
    common_shape = (N_DP, 1, KEY_HEADS, 1, HEAD_SIZE)
    base = jax.random.truncated_normal(first, -6.0, 6.0, array_shape, jnp.float32)
    common = 3.0 * jax.random.truncated_normal(fourth_item, -6.0, 6.0, common_shape, jnp.float32)
    noise_keys = base[:, :, 0]
    values = 2.0 * base[:, :, 1]
    spread_common = jnp.broadcast_to(common, (N_DP, OWNER_PAGES, KEY_HEADS, PAGE_TOKENS, HEAD_SIZE))
    keys = noise_keys + spread_common.reshape(N_DP * OWNER_PAGES, KEY_HEADS, PAGE_TOKENS, HEAD_SIZE)
    combined_rows = jnp.stack([keys, values], axis=2)
    return combined_rows.reshape(N_DP * OWNER_PAGES, 2 * KEY_HEADS, PAGE_TOKENS, HEAD_SIZE).astype(jnp.bfloat16)


def draw_prompt_pages(key, part):
    key = jax.random.fold_in(key, 11)
    first, second_item, third_item = jax.random.split(key, 3)
    count = N_DP * PR_DEV
    values = jax.random.randint(first, (count,), 1, LONGEST_PAGES + 1, jnp.int32)
    spot = jax.random.randint(second_item, (), 0, count, jnp.int32)
    other = (spot + 1 + jax.random.randint(third_item, (), 0, count - 1, jnp.int32)) % count
    places = jnp.arange(count, dtype=jnp.int32)
    values = jnp.where(places == spot, LONGEST_PAGES, values)
    values = jnp.where(places == other, 1, values)
    return values.reshape(N_DP, PR_DEV)


def level_of(rng, dims, cuts, smallest, top_value):
    level, own = 1.0, jax.random.fold_in(rng, 6)
    for dim, shards_of in cuts:
        draws = jnp.exp(jax.random.uniform(jax.random.fold_in(own, dim), (shards_of,), jnp.float32, smallest / len(cuts), top_value / len(cuts)))
        level = level * jnp.repeat(draws, dims[dim] // shards_of).reshape([-1 if axis == dim else 1 for axis in range(len(dims))])
    return level


def length_profile(count, total, most, slope):
    portions = [(1 << 20) // math.isqrt(standing ** slope) + 1 for standing in range(2, count + 1)]
    surplus, given = total - most - (count - 1), [1] * (count - 1)
    while surplus > 0:
        free = [i for i in range(count - 1) if given[i] < most]
        mass, remaining = sum([portions[i] for i in free]), surplus
        for i in free:
            more = min(most - given[i], max(1, remaining * portions[i] // mass), surplus)
            given[i] = given[i] + more
            surplus = surplus - more
    return np.array([most] + given)


def uneven_parts(key, amount, total, bound, skew):
    if amount == 2:
        one = jax.random.randint(key, (), max(1, total - bound), min(bound, total - 1) + 1)
        return jnp.stack([one, total - one])
    sizes = jnp.asarray(length_profile(amount, total, bound, skew), jnp.int32)
    twos = (amount - 1) // 2
    source_of, taker = sizes[1:1 + 2 * twos:2], sizes[2:2 + 2 * twos:2]
    room = jnp.minimum(source_of - 1, bound - taker)
    passed = jax.random.randint(jax.random.fold_in(key, 1), (twos,), 0, 1 << 20) % (room + 1)
    sizes = sizes.at[1:1 + 2 * twos:2].set(source_of - passed).at[2:2 + 2 * twos:2].set(taker + passed)
    return sizes[jax.random.permutation(jax.random.fold_in(key, 2), amount)]


def normal_values(stream_key, dims, spread, most, shards=(), kind=jnp.bfloat16):
    drawn = jax.random.normal(stream_key, dims, jnp.float32) * spread
    if len(shards) > 0:
        drawn = level_of(stream_key, dims, shards, -0.22, 0.18) * drawn
    return jnp.clip(drawn, min=-most, max=most).astype(kind)


def setup_inputs(seed: int = 0) -> dict:
    splits = jax.random.split(jax.random.key(seed), 9)
    return {
        "new_states": normal_values(splits[0], (ROWS, DECODE_STEPS, MODEL_WIDTH), 1.0, 6.0, ((0, 256),)),
        "w_query": normal_values(splits[1], (MODEL_WIDTH, QUERY_HEADS * HEAD_SIZE), MODEL_WIDTH ** -0.5, 0.078125, ((1, 8),)),
        "keyvalue_weight": normal_values(splits[2], (MODEL_WIDTH, 2 * KEY_HEADS, HEAD_SIZE), MODEL_WIDTH ** -0.5, 0.078125, ((1, 8),)),
        "keyvalue_pages": draw_keyvalue_pages(jax.random.fold_in(splits[8], 71), 0),
        "page_table": jax.vmap(lambda own: jax.random.permutation(own, OWNER_PAGES))(jax.random.split(splits[4], N_DP)).reshape((N_DP, OWNER_PAGES)).astype(jnp.int32),
        "prompt_pages": draw_prompt_pages(jax.random.fold_in(splits[8], 71), 0),
        "share_prompt": jax.vmap(lambda own: jnp.searchsorted(jnp.cumsum(uneven_parts(own, PR_DEV, N_DP, 8, 2)), jnp.arange(N_DP), side="right"))(jax.random.split(splits[6], N_DP)).reshape((N_DP, N_DP)).astype(jnp.int32),
        "share_group": jax.vmap(lambda own: jax.random.permutation(own, N_DP))(jax.random.split(splits[7], N_DP)).reshape((N_DP, N_DP)).astype(jnp.int32),
    }


def head_norm(values):
    values = values.astype(jnp.float32)
    return values * lax.rsqrt(lax.optimization_barrier(jnp.mean(values * values, axis=-1, keepdims=True)) + 1e-06)

def rotary(values, positions):
    half = values.shape[-1] // 2
    freqs = jnp.exp(-(2.0 * jnp.arange(half, dtype=jnp.float32) / values.shape[-1]) * jnp.log(1000000.0))
    angles = positions.astype(jnp.float32)[..., None] * freqs
    cosine = jnp.cos(angles)
    sine = jnp.sin(angles)
    first = values[..., :half]
    second_item = values[..., half:]
    return jnp.concatenate([first * cosine - second_item * sine, second_item * cosine + first * sine], axis=-1)

def prompt_part(queries, keys, values, page_counts):
    width = queries.shape[-1]
    scores = jnp.einsum('osthgd,omhpd->osthgmp', queries.astype(jnp.float32), keys.astype(jnp.float32)) * (1.0 / math.sqrt(width))
    valid = jnp.arange(keys.shape[1], dtype=jnp.int32)[None, :] < page_counts[:, None]
    valid = valid.reshape(valid.shape[0], 1, 1, 1, 1, valid.shape[1], 1)
    peak = lax.optimization_barrier(jnp.max(jnp.where(valid, scores, -jnp.inf), axis=(5, 6)))
    weights = jnp.where(valid, jnp.exp(scores - peak[..., None, None]), 0.0)
    total = lax.optimization_barrier(jnp.sum(weights, axis=(5, 6)))
    rounded = weights.astype(jnp.bfloat16).astype(jnp.float32)
    numer = jnp.einsum('osthgmp,omhpd->osthgd', rounded, values.astype(jnp.float32))
    return (numer, peak, total)

def newest_portion(queries, keys, values):
    width = queries.shape[-1]
    steps = queries.shape[2]
    scores = jnp.einsum('osthgd,osuhd->osthgu', queries.astype(jnp.float32), keys.astype(jnp.float32)) * (1.0 / math.sqrt(width))
    causal = jnp.arange(steps)[:, None] >= jnp.arange(steps)[None, :]
    causal = causal.reshape(1, 1, steps, 1, 1, steps)
    peak = lax.optimization_barrier(jnp.max(jnp.where(causal, scores, -jnp.inf), axis=5))
    weights = jnp.where(causal, jnp.exp(scores - peak[..., None]), 0.0)
    total = lax.optimization_barrier(jnp.sum(weights, axis=5))
    rounded = weights.astype(jnp.bfloat16).astype(jnp.float32)
    numer = jnp.einsum('osthgu,osuhd->osthgd', rounded, values.astype(jnp.float32))
    return (numer, peak, total)

def reference(new_states, w_query, keyvalue_weight, keyvalue_pages, page_table, prompt_pages, share_prompt, share_group):
    prefill_owners = N_DP
    group_query = QUERY_HEADS // KEY_HEADS
    targets = jnp.arange(prefill_owners, dtype=jnp.int32)
    match = (share_group[:, :, None] == targets[None, None, :]).astype(jnp.int32)
    slot_prompt = lax.optimization_barrier(jnp.sum(match * share_prompt[:, :, None], axis=1))
    choose = (slot_prompt[:, :, None] == jnp.arange(PR_DEV, dtype=jnp.int32)[None, None, :]).astype(jnp.int32)
    slot_pages = lax.optimization_barrier(jnp.sum(choose * prompt_pages[:, None, :], axis=2))
    base = (jnp.arange(prefill_owners, dtype=jnp.int32) * OWNER_PAGES)[:, None]

    def one_group(group):
        rows = lax.dynamic_slice_in_dim(new_states, (group * GROUP_SAMPLES).astype(jnp.int32), GROUP_SAMPLES, 0)
        flat = rows.reshape(-1, MODEL_WIDTH).astype(jnp.float32)
        normalized_output = (flat * lax.rsqrt(lax.optimization_barrier(jnp.mean(flat * flat, axis=-1, keepdims=True)) + 1e-06)).astype(jnp.bfloat16)
        raw_query = jnp.dot(normalized_output, w_query, preferred_element_type=jnp.float32).reshape(GROUP_SAMPLES, DECODE_STEPS, QUERY_HEADS, HEAD_SIZE)
        unrotated_keyvalue = jnp.dot(normalized_output, keyvalue_weight.reshape(MODEL_WIDTH, -1), preferred_element_type=jnp.float32).reshape(GROUP_SAMPLES, DECODE_STEPS, KEY_HEADS, 2 * HEAD_SIZE)
        counts = slot_pages[:, group]
        positions = PAGE_TOKENS * counts[:, None, None] + jnp.zeros((prefill_owners, PROMPT_SAMPLES, DECODE_STEPS), jnp.int32) + jnp.arange(DECODE_STEPS, dtype=jnp.int32)[None, None, :]
        positions = positions.reshape(GROUP_SAMPLES, DECODE_STEPS, 1)
        query_vector = rotary(head_norm(raw_query), positions).astype(jnp.bfloat16)
        latest_key = rotary(head_norm(unrotated_keyvalue[..., :HEAD_SIZE]), positions).astype(jnp.bfloat16)
        latest_value = unrotated_keyvalue[..., HEAD_SIZE:].astype(jnp.bfloat16)
        logical = slot_prompt[:, group][:, None] * LONGEST_PAGES + jnp.arange(LONGEST_PAGES, dtype=jnp.int32)[None, :]
        physical_pages = jnp.take_along_axis(page_table, logical.astype(jnp.int32), axis=1) + base
        page_list = keyvalue_pages[physical_pages].reshape(prefill_owners, LONGEST_PAGES, KEY_HEADS, 2, PAGE_TOKENS, HEAD_SIZE)
        block_list = query_vector.reshape(prefill_owners, PROMPT_SAMPLES, DECODE_STEPS, KEY_HEADS, group_query, HEAD_SIZE)
        numer_p, peak_p, total_p = prompt_part(block_list, page_list[:, :, :, 0], page_list[:, :, :, 1], counts)
        numerator_running, running_maximum, running_total = newest_portion(block_list, latest_key.reshape(prefill_owners, PROMPT_SAMPLES, DECODE_STEPS, KEY_HEADS, HEAD_SIZE), latest_value.reshape(prefill_owners, PROMPT_SAMPLES, DECODE_STEPS, KEY_HEADS, HEAD_SIZE))
        top = jnp.maximum(peak_p, running_maximum)
        first = jnp.exp(peak_p - top)
        second_item = jnp.exp(running_maximum - top)
        merged = (numer_p * first[..., None] + numerator_running * second_item[..., None]) / (total_p * first + running_total * second_item)[..., None]
        return merged.reshape(GROUP_SAMPLES, DECODE_STEPS, QUERY_HEADS * HEAD_SIZE).astype(jnp.bfloat16)
    result = lax.map(one_group, jnp.arange(prefill_owners, dtype=jnp.int32))
    return result.reshape(ROWS, DECODE_STEPS, QUERY_HEADS * HEAD_SIZE)
```

```python
import functools
import math

import jax
import jax.numpy as jnp
from jax import lax
from jax.experimental import pallas as pl
from jax.experimental.pallas import tpu as pltpu
from jax.sharding import PartitionSpec as P

HEAD_SIZE = 128
PAGE_TOKENS = 128
LONGEST_PAGES = 4
PROMPT_SAMPLES = 8
STEPS = 4
EPSILON = 1e-06

Y, Z, X, C = 4, 8, 4, 2
SLAB = PROMPT_SAMPLES * STEPS
PARTS = 2
SLOTS = 8
STAT_ROWS = 16
MiB = 1024 * 1024


def rank(y, z, x, c):
    return (y * Z + z) * X * C + x * C + c


def everywhere(target):
    pairs = []
    for y in range(Y):
        for z in range(Z):
            for x in range(X):
                for c in range(C):
                    a, b = z // 4, z % 4
                    pairs.append((rank(y, z, x, c), rank(*target(y, a, b, x, c))))
    return pairs


def along_x(step):
    return [(x * C + c, (x + step) % X * C + c) for x in range(X) for c in range(C)]


def other_core():
    return [(i, i ^ 1) for i in range(X * C)]


def along_y(step):
    return [(y * Z + z, (y + step) % Y * Z + z) for y in range(Y) for z in range(Z)]


def along_z(kappa):
    return everywhere(lambda y, a, b, x, c: (y, 4 * c + (b ^ kappa), x, a))


def coordinates():
    d = lax.axis_index("dp")
    t = lax.axis_index("tensor")
    z = d % Z
    return d // Z, z // 4, z % 4, t // C, t % C


def rope_tables():
    half = HEAD_SIZE // 2
    freqs = jnp.exp(
        -(2.0 * jnp.arange(half, dtype=jnp.float32) / HEAD_SIZE) * jnp.log(1000000.0)
    )
    pages = jnp.arange(1, LONGEST_PAGES + 1, dtype=jnp.int32)[:, None]
    steps = jnp.arange(2 * STEPS, dtype=jnp.int32)[None, :] % STEPS
    angles = (PAGE_TOKENS * pages + steps).astype(jnp.float32)[..., None] * freqs
    cosine, sine = jnp.cos(angles), jnp.sin(angles)
    return (
        jnp.concatenate([cosine, cosine], axis=-1),
        jnp.concatenate([-sine, sine], axis=-1),
    )


def norm_kernel(part, place, *refs):
    states, (slab, token, held, scratch, sem) = refs[0], refs[-5:]
    token[...] = jnp.zeros_like(token)
    high = (place[2] >> 1) ^ part
    load = pltpu.make_async_copy(
        states.at[pl.ds(high * 2 * PROMPT_SAMPLES, 2 * PROMPT_SAMPLES)], held, sem
    )
    load.start()
    load.wait()
    for r in range(2 * PROMPT_SAMPLES):
        flat = held[r].astype(jnp.float32)
        flat = flat * lax.rsqrt(jnp.mean(flat * flat, axis=-1, keepdims=True) + EPSILON)
        scratch[r * STEPS:(r + 1) * STEPS, :] = flat
    slab[...] = scratch[...].astype(jnp.bfloat16)


def forward_kernel(ahead, behind, *refs):
    far_0, far_1, token, sems = refs[-4:]
    token[...] = jnp.zeros_like(token)
    copies = [
        pltpu.make_async_copy(ahead.at[pl.ds(0, SLAB)], far_0, sems.at[0]),
        pltpu.make_async_copy(behind.at[pl.ds(SLAB, SLAB)], far_1, sems.at[1]),
    ]
    for copy in copies:
        copy.start()
    for copy in copies:
        copy.wait()


def pack_kernel(m_0, m_1, m_2, m_3, after, low_0, low_1, token):
    for jy, moved in enumerate((m_0, m_1, m_2, m_3)):
        low_0[jy] = moved[0]
        low_1[jy] = moved[1]
    token[...] = jnp.zeros_like(token)


def repack_kernel(r_0, r_1, after, b_0, b_1, b_2, b_3, token):
    for jy, back in enumerate((b_0, b_1, b_2, b_3)):
        back[0] = r_0[jy]
        back[1] = r_1[jy]
    token[...] = jnp.zeros_like(token)


def slot_pages_of(place, counts, part, delta, low):
    b, x, c = place[2], place[3], place[4]
    owner = Z * ((x + delta) % X) + 4 * c + ((b & 2) ^ (2 * part)) + low
    return counts[owner]


def rotated(values, cosine, sine):
    values = values * lax.rsqrt(jnp.mean(values * values, axis=-1, keepdims=True) + EPSILON)
    turned = pltpu.roll(values, HEAD_SIZE // 2, 1)
    fold = (SLAB // 8, 8, HEAD_SIZE)
    out = values.reshape(fold) * cosine[None] + turned.reshape(fold) * sine[None]
    return out.reshape(SLAB, HEAD_SIZE)


def project_kernel(part, place, counts, *refs):
    slabs, refs = refs[:-15], refs[-15:]
    sources, (cos_ref, sin_ref, after), outs = refs[:4], refs[4:7], refs[7:11]
    kept, keys, values_ref, sent = refs[11:]
    y, b, x = place[0], place[2], place[3]
    states = jnp.concatenate([slab[...] for slab in slabs], axis=0)
    tables = []
    for slot in range(SLOTS):
        n = slot_pages_of(place, counts, part, slot // 2, slot % 2)
        tables.append((cos_ref[n - 1], sin_ref[n - 1]))
    for block in range(4):
        which = block // 2
        raw = jnp.dot(
            states, sources[which][:, block % 2 * 256:block % 2 * 256 + 256],
            preferred_element_type=jnp.float32,
        )
        for slot in range(SLOTS):
            jy, low = (x + slot // 2 - y + Y) % Y, (slot % 2) ^ (b & 1)
            for head in range(2):
                query = raw[slot * SLAB:(slot + 1) * SLAB, head * HEAD_SIZE:(head + 1) * HEAD_SIZE]
                query = rotated(query, *tables[slot]).astype(jnp.bfloat16)
                at = pl.ds((block % 2 * 2 + head) * SLAB, SLAB)
                kept[slot, which, at, :] = query
                sent[jy, low, which, at, :] = query
    for which in range(2):
        raw = jnp.dot(states, sources[2 + which][...], preferred_element_type=jnp.float32)
        for slot in range(SLOTS):
            rows = raw[slot * SLAB:(slot + 1) * SLAB]
            keys[slot, which] = rotated(rows[:, :HEAD_SIZE], *tables[slot]).astype(jnp.bfloat16)
            values_ref[slot, which] = rows[:, HEAD_SIZE:].astype(jnp.bfloat16)
    for jy in range(Y):
        outs[jy][...] = sent[jy]


def newest_kernel(kept, keys, values, after, numer_ref, stat_ref, token_ref):
    token_ref[...] = jnp.zeros_like(token_ref)
    token = lax.broadcasted_iota(jnp.int32, (SLAB, 4 * SLAB), 0)
    line = lax.broadcasted_iota(jnp.int32, (SLAB, 4 * SLAB), 1) % SLAB
    seen = (line // STEPS == token // STEPS) & (token <= line)
    for which in range(2):
        scores = [
            lax.dot_general(
                keys[slot, which], kept[slot, which], (((1,), (1,)), ((), ())),
                preferred_element_type=jnp.float32,
            )
            for slot in range(SLOTS)
        ]
        mass = []
        for slot in range(SLOTS):
            score = jnp.where(seen, scores[slot] * (1.0 / math.sqrt(HEAD_SIZE)), -jnp.inf)
            peak = jnp.max(score, axis=0, keepdims=True)
            mass.append(jnp.exp(score - peak))
            stat_ref[slot, which, 0:1, :] = peak
            stat_ref[slot, which, 1:2, :] = jnp.sum(mass[-1], axis=0, keepdims=True)
        for slot in range(SLOTS):
            numer_ref[slot, which] = jnp.dot(
                mass[slot].T.astype(jnp.bfloat16), values[slot, which],
                preferred_element_type=jnp.float32,
            )


def diagonal():
    first = lax.broadcasted_iota(jnp.int32, (4 * SLAB, HEAD_SIZE), 0)
    return first == lax.broadcasted_iota(jnp.int32, (4 * SLAB, HEAD_SIZE), 1)


def prompt_kernel(part, place, tables, counts, q_0, q_1, own, other, after, out_0, out_1, token_ref):
    token_ref[...] = jnp.zeros_like(token_ref)
    y, a, b, c = place[0], place[1], place[2], place[4]
    eye = diagonal()
    row = lax.broadcasted_iota(jnp.int32, (STAT_ROWS, HEAD_SIZE), 0)
    token = lax.broadcasted_iota(jnp.int32, (4 * SLAB, LONGEST_PAGES * PAGE_TOKENS), 1)
    scale = math.log2(math.e) / math.sqrt(HEAD_SIZE)

    def one(jy, carry):
        group = [Z * ((y - jy + Y) % Y) + 4 * c + (b ^ (2 * part + low)) for low in range(2)]
        at = [[tables[g * LONGEST_PAGES + page] for page in range(LONGEST_PAGES)] for g in group]
        valid = [token < counts[g] * PAGE_TOKENS for g in group]
        tiles = [(low, which, which ^ a ^ c) for low in range(2) for which in range(2)]
        scores = []
        for low, which, head in tiles:
            keys = jnp.concatenate([(own, other)[which][p, 0] for p in at[low]], axis=0)
            scores.append(
                lax.dot_general(
                    (q_0, q_1)[low][jy, head], keys, (((1,), (1,)), ((), ())),
                    preferred_element_type=jnp.float32,
                )
            )
        mass, total, logs = [], [], []
        for (low, which, head), score in zip(tiles, scores):
            score = jnp.where(valid[low], score, -jnp.inf)
            peak = jnp.max(score, axis=-1, keepdims=True)
            mass.append(jnp.exp2((score - peak) * scale))
            total.append(jnp.sum(mass[-1], axis=-1, keepdims=True))
            logs.append(peak * (1.0 / math.sqrt(HEAD_SIZE)) + jnp.log(total[-1]))
        stats = [jnp.zeros((STAT_ROWS, HEAD_SIZE), jnp.float32)] * 2
        for tile, (low, which, head) in enumerate(tiles):
            values = jnp.concatenate([(own, other)[which][p, 1] for p in at[low]], axis=0)
            numer = jnp.dot(
                mass[tile].astype(jnp.bfloat16), values, preferred_element_type=jnp.float32
            )
            first = pl.multiple_of(head * 4 * SLAB, 4 * SLAB)
            (out_0, out_1)[low][jy, pl.ds(first, 4 * SLAB), :] = (numer / total[tile]).astype(
                jnp.bfloat16
            )
            flat = jnp.sum(jnp.where(eye, logs[tile], 0.0), axis=0, keepdims=True)
            for piece in range(3):
                rounded = flat.astype(jnp.bfloat16).astype(jnp.float32)
                stats[low] = jnp.where(row == 3 * head + piece, rounded, stats[low])
                flat = flat - rounded
        for low in range(2):
            (out_0, out_1)[low][jy, pl.ds(8 * SLAB, STAT_ROWS), :] = stats[low].astype(jnp.bfloat16)
        return carry

    lax.fori_loop(0, Y, one, 0)


def merge_kernel(place, r_0, r_1, r_2, r_3, numer_ref, stat_ref, after, own_ref, other_ref):
    y, b, x = place[0], place[2], place[3]
    eye = diagonal()
    for slot in range(SLOTS):
        jy = slot // 2
        back, owner_y, low = (r_0, r_1, r_2, r_3)[jy], (y + jy) % Y, (slot % 2) ^ (b & 1)
        kept = (owner_y - x + X) % X * 2 + low
        stats = back[slot % 2, pl.ds(8 * SLAB, STAT_ROWS), :].astype(jnp.float32)
        for head in range(2):
            log_p = stats[3 * head:3 * head + 1] + (
                stats[3 * head + 1:3 * head + 2] + stats[3 * head + 2:3 * head + 3]
            )
            newest = stat_ref[kept, head]
            peak_n, total_n = newest[0:1], newest[1:2]
            log_n = peak_n + jnp.log(total_n)
            top = jnp.maximum(log_p, log_n)
            first, second = jnp.exp(log_p - top), jnp.exp(log_n - top)
            share_p = first / (first + second)
            share_n = second / ((first + second) * total_n)
            share_p = jnp.sum(jnp.where(eye, share_p, 0.0), axis=1, keepdims=True)
            share_n = jnp.sum(jnp.where(eye, share_n, 0.0), axis=1, keepdims=True)
            prompt = back[slot % 2, pl.ds(head * 4 * SLAB, 4 * SLAB), :].astype(jnp.float32)
            merged = (prompt * share_p + numer_ref[kept, head] * share_n).astype(jnp.bfloat16)
            out = (own_ref, other_ref)[head]
            for j in range(4):
                out[owner_y, low, :, pl.ds(j * HEAD_SIZE, HEAD_SIZE)] = merged[
                    j * SLAB:(j + 1) * SLAB
                ]


def assemble_kernel(place, *refs):
    b, c = place[2], place[4]
    sources, out = refs[:-1], refs[-1]
    for part in range(PARTS):
        high = (b >> 1) ^ part
        for which in range(2):
            for owner_y in range(Y):
                out[owner_y, c ^ which, high] = sources[2 * part + which][owner_y]


VMEM = pl.BlockSpec(memory_space=pltpu.VMEM)
SMEM = pl.BlockSpec(memory_space=pltpu.SMEM)
HBM = pl.BlockSpec(memory_space=pltpu.HBM)
ANY = pl.BlockSpec(memory_space=pl.ANY)
TOKEN = jax.ShapeDtypeStruct((8, 128), jnp.float32)


def params(mib):
    return pltpu.CompilerParams(vmem_limit_bytes=mib * MiB)


def body(
    new_states,
    w_query,
    keyvalue_weight,
    keyvalue_pages,
    page_table,
    prompt_pages,
    share_prompt,
    share_group,
):
    groups = lax.axis_size("dp")
    width = new_states.shape[2]
    y, a, b, x, c = coordinates()
    place = jnp.stack([y, a, b, x, c]).astype(jnp.int32)

    targets = jnp.arange(groups, dtype=jnp.int32)
    match = (share_group[0][:, None] == targets[None, :]).astype(jnp.int32)
    dest_prompt = jnp.sum(match * share_prompt[0][:, None], axis=0)
    choose = (
        dest_prompt[:, None] == jnp.arange(prompt_pages.shape[1], dtype=jnp.int32)[None, :]
    ).astype(jnp.int32)
    dest_count = jnp.sum(choose * prompt_pages[0][None, :], axis=1)
    logical = (
        dest_prompt[:, None] * LONGEST_PAGES + jnp.arange(LONGEST_PAGES, dtype=jnp.int32)[None, :]
    )
    lookup = (
        logical[:, :, None] == jnp.arange(page_table.shape[1], dtype=jnp.int32)[None, None, :]
    ).astype(jnp.int32)
    physical = jnp.sum(lookup * page_table[0][None, None, :], axis=2).reshape(-1)
    slot_count = lax.all_to_all(dest_count, "dp", split_axis=0, concat_axis=0, tiled=True)
    cosine, sine = rope_tables()

    wq_other = lax.ppermute(w_query, "tensor", other_core())

    slab = jax.ShapeDtypeStruct((SLAB, width), jnp.bfloat16)

    def norm(part, after):
        own, token = pl.pallas_call(
            functools.partial(norm_kernel, part),
            out_shape=(jax.ShapeDtypeStruct((2 * SLAB, width), jnp.bfloat16), TOKEN),
            in_specs=[SMEM, HBM] + [VMEM] * len(after),
            out_specs=(VMEM,) * 2,
            scratch_shapes=[
                pltpu.VMEM((2 * PROMPT_SAMPLES, STEPS, width), jnp.bfloat16),
                pltpu.VMEM((2 * SLAB, width), jnp.float32),
                pltpu.SemaphoreType.DMA,
            ],
            compiler_params=params(8),
            name="norm",
        )(place, new_states, *after)
        ahead = lax.ppermute(own, "tensor", along_x(1))
        behind = lax.ppermute(own, "tensor", along_x(-1))
        return own, ahead, behind, token

    def forward(own, ahead, behind, *after):
        far_0, far_1, token = pl.pallas_call(
            forward_kernel,
            out_shape=(slab, slab, TOKEN),
            in_specs=[ANY] * 2 + [VMEM if a.ndim > 1 else SMEM for a in after],
            out_specs=(VMEM,) * 3,
            scratch_shapes=[pltpu.SemaphoreType.DMA((2,))],
            compiler_params=params(4),
            name="forward",
        )(ahead, behind, *after)
        far_0 = lax.ppermute(far_0, "tensor", along_x(1))
        far_1 = lax.ppermute(far_1, "tensor", along_x(-1))
        return (own, behind, far_0, far_1, ahead), token

    pages_other = lax.ppermute(keyvalue_pages, "tensor", other_core())
    *rows, _ = norm(0, ())
    piece, token = forward(*rows, slot_count, wq_other[:8, :128], pages_other[0, 0, :8])
    pieces = [piece]
    *rows, _ = norm(1, (piece[2][:8, :128], piece[3][:8, :128]))
    wkv = keyvalue_weight.reshape(width, -1) + token[0, 0].astype(jnp.bfloat16)
    wkv_other = lax.ppermute(wkv, "tensor", other_core())

    def project(part, after):
        message = jax.ShapeDtypeStruct((2, 2, 4 * SLAB, HEAD_SIZE), jnp.bfloat16)
        kept = jax.ShapeDtypeStruct((SLOTS, 2, 4 * SLAB, HEAD_SIZE), jnp.bfloat16)
        pair = jax.ShapeDtypeStruct((SLOTS, 2, SLAB, HEAD_SIZE), jnp.bfloat16)
        sources = (w_query, wq_other, wkv, wkv_other)
        *queries, kept, keys, values = pl.pallas_call(
            functools.partial(project_kernel, part),
            out_shape=(message,) * Y + (kept, pair, pair),
            in_specs=[SMEM] * 2 + [VMEM] * (len(pieces[part]) + 7),
            out_specs=(VMEM,) * (Y + 3),
            scratch_shapes=[pltpu.VMEM((Y, 2, 2, 4 * SLAB, HEAD_SIZE), jnp.bfloat16)],
            compiler_params=params(28),
            name="project",
        )(place, slot_count, *pieces[part], *sources, cosine, sine, after)
        moved = [queries[0]] + [lax.ppermute(queries[j], "dp", along_y(j)) for j in range(1, Y)]
        return moved, (kept, keys, values)

    def newest(part, rows, after):
        return pl.pallas_call(
            newest_kernel,
            out_shape=(
                jax.ShapeDtypeStruct((SLOTS, 2, 4 * SLAB, HEAD_SIZE), jnp.float32),
                jax.ShapeDtypeStruct((SLOTS, 2, 8, 4 * SLAB), jnp.float32),
                TOKEN,
            ),
            in_specs=[VMEM] * 4,
            out_specs=(VMEM,) * 3,
            compiler_params=params(8),
            name="newest_tokens",
        )(*rows, after)

    def pack(part, moved, after):
        message = jax.ShapeDtypeStruct((Y, 2, 4 * SLAB, HEAD_SIZE), jnp.bfloat16)
        *packed, token = pl.pallas_call(
            pack_kernel,
            out_shape=(message,) * 2 + (TOKEN,),
            in_specs=[VMEM] * 5,
            out_specs=(VMEM,) * 3,
            compiler_params=params(4),
            name="pack",
        )(*moved, after)
        asked = [
            lax.ppermute(packed[low], ("dp", "tensor"), along_z(2 * part + low)) for low in range(2)
        ]
        return asked, token

    def answer(part, asked, after):
        message = jax.ShapeDtypeStruct((Y, 8 * SLAB + STAT_ROWS, HEAD_SIZE), jnp.bfloat16)
        *answers, token = pl.pallas_call(
            functools.partial(prompt_kernel, part),
            out_shape=(message,) * 2 + (TOKEN,),
            in_specs=[SMEM] * 3 + [VMEM] * 5,
            out_specs=(VMEM,) * 3,
            compiler_params=params(8),
            name="prompt_attention",
        )(place, physical, dest_count, *asked, keyvalue_pages, pages_other, after)
        returned = [
            lax.ppermute(answers[low], ("dp", "tensor"), along_z(2 * part + low)) for low in range(2)
        ]
        return returned, token

    def repack(returned, after):
        message = jax.ShapeDtypeStruct((2, 8 * SLAB + STAT_ROWS, HEAD_SIZE), jnp.bfloat16)
        *back, token = pl.pallas_call(
            repack_kernel,
            out_shape=(message,) * Y + (TOKEN,),
            in_specs=[VMEM] * 3,
            out_specs=(VMEM,) * (Y + 1),
            compiler_params=params(4),
            name="repack",
        )(*returned, after)
        back = [back[0]] + [lax.ppermute(back[j], "dp", along_y(-j)) for j in range(1, Y)]
        return back, token

    def merge(back, new_part, after):
        half = jax.ShapeDtypeStruct((Y, 2, SLAB, 4 * HEAD_SIZE), jnp.bfloat16)
        mine, theirs = pl.pallas_call(
            merge_kernel,
            out_shape=(half,) * 2,
            in_specs=[SMEM] + [VMEM] * 7,
            out_specs=(VMEM,) * 2,
            compiler_params=params(8),
            name="merge",
        )(place, *back, *new_part[:2], after)
        return [mine, lax.ppermute(theirs, "tensor", other_core())]

    moved_0, rows_0 = project(0, cosine)
    piece, token = forward(*rows, rows_0[1])
    pieces.append(piece)
    new_0 = newest(0, rows_0, token)
    asked_0, token = pack(0, moved_0, new_0[2])
    moved_1, rows_1 = project(1, token)
    returned_0, token = answer(0, asked_0, rows_1[1])
    asked_1, token = pack(1, moved_1, token)
    new_1 = newest(1, rows_1, token)
    back_0, token = repack(returned_0, new_1[2])
    returned_1, token = answer(1, asked_1, token)
    ends = merge(back_0, new_0, token)
    back_1, token = repack(returned_1, token)
    ends += merge(back_1, new_1, token)

    out = pl.pallas_call(
        assemble_kernel,
        out_shape=jax.ShapeDtypeStruct((Y, 2, 2, 2, SLAB, 4 * HEAD_SIZE), jnp.bfloat16),
        in_specs=[SMEM] + [VMEM] * (2 * PARTS),
        out_specs=VMEM,
        compiler_params=params(8),
        name="assemble",
    )(place, *ends)
    return out.reshape(groups * PROMPT_SAMPLES, STEPS, 4 * HEAD_SIZE)


def solution(mesh):
    placed = (
        P(("dp", "tensor"), None, None),
        P(None, "tensor"),
        P(None, "tensor", None),
        P("dp", "tensor", None, None),
        P("dp", None),
        P("dp", None),
        P("dp", None),
        P("dp", None),
    )
    return jax.shard_map(
        body, mesh=mesh, in_specs=placed, out_specs=P("dp", None, "tensor"), check_vma=False
    )
```

```python
import functools
import math

import jax
import jax.numpy as jnp
from jax import lax
from jax.experimental import pallas as pl
from jax.experimental.pallas import tpu as pltpu
from jax.sharding import PartitionSpec as P

HEAD_SIZE = 128
PAGE_TOKENS = 128
LONGEST_PAGES = 4
PROMPT_SAMPLES = 8
STEPS = 4
EPSILON = 1e-06

Y, Z, X, C = 4, 8, 4, 2
SLAB = PROMPT_SAMPLES * STEPS
OWNERS = 32
HEADS = 4
TILE = HEADS * SLAB
STAT_ROWS = 16
MiB = 1024 * 1024


def along_x(step):
    return [(x * C + c, (x + step) % X * C + c) for x in range(X) for c in range(C)]


def other_core():
    return [(i, i ^ 1) for i in range(X * C)]


def rope_tables():
    half = HEAD_SIZE // 2
    freqs = jnp.exp(
        -(2.0 * jnp.arange(half, dtype=jnp.float32) / HEAD_SIZE) * jnp.log(1000000.0)
    )
    pages = jnp.arange(1, LONGEST_PAGES + 1, dtype=jnp.int32)[:, None]
    steps = jnp.arange(2 * STEPS, dtype=jnp.int32)[None, :] % STEPS
    angles = (PAGE_TOKENS * pages + steps).astype(jnp.float32)[..., None] * freqs
    cosine, sine = jnp.cos(angles), jnp.sin(angles)
    return (
        jnp.concatenate([cosine, cosine], axis=-1),
        jnp.concatenate([-sine, sine], axis=-1),
    )


def rotated(values, cosine, sine):
    values = values * lax.rsqrt(jnp.mean(values * values, axis=-1, keepdims=True) + EPSILON)
    turned = pltpu.roll(values, HEAD_SIZE // 2, 1)
    fold = (SLAB // 8, 8, HEAD_SIZE)
    out = values.reshape(fold) * cosine[None] + turned.reshape(fold) * sine[None]
    return out.reshape(SLAB, HEAD_SIZE)


def norm_kernel(states, slab, held, scratch, sem):
    load = pltpu.make_async_copy(states, held, sem)
    load.start()
    load.wait()
    for r in range(states.shape[0]):
        flat = held[r].astype(jnp.float32)
        flat = flat * lax.rsqrt(jnp.mean(flat * flat, axis=-1, keepdims=True) + EPSILON)
        scratch[r * STEPS:(r + 1) * STEPS, :] = flat
    slab[...] = scratch[...].astype(jnp.bfloat16)


def forward_kernel(ahead, behind, *refs):
    both, far_0, far_1 = refs[-3:]
    half = ahead.shape[0] // 2
    both[:2 * half] = behind[...]
    both[2 * half:] = ahead[...]
    far_0[...] = ahead[:half]
    far_1[...] = behind[half:]


def join_kernel(far_0, far_1, after, far):
    half = far_0.shape[0]
    far[:half] = far_0[...]
    far[half:] = far_1[...]


def project(place, counts, deltas, mine, theirs, wq, wkv, cos_ref, sin_ref, put):
    x, c = place[0], place[1]
    states = jnp.concatenate([mine, theirs], axis=0)
    slots = []
    for side in range(2):
        for number, delta in enumerate(deltas):
            for j in range(4):
                within = 4 * (c ^ side) + j
                n = counts[Z * ((x + delta) % X) + within]
                slots.append((number, within, cos_ref[n - 1], sin_ref[n - 1]))
    for block in range(3):
        weight = wq[:, block * 256:block * 256 + 256] if block < 2 else wkv[...]
        raw = jnp.dot(states, weight, preferred_element_type=jnp.float32)
        for slot, (number, within, cosine, sine) in enumerate(slots):
            rows = raw[slot * SLAB:(slot + 1) * SLAB]
            first, second = rows[:, :HEAD_SIZE], rows[:, HEAD_SIZE:]
            first = rotated(first, cosine, sine).astype(jnp.bfloat16)
            if block < 2:
                second = rotated(second, cosine, sine)
            second = second.astype(jnp.bfloat16)
            put(number, within, 2 * block, first)
            put(number, within, 2 * block + 1, second)


def near_kernel(deltas, place, counts, *refs):
    slabs, (wq, wkv, cos_ref, sin_ref, near) = refs[:-5], refs[-5:]

    def put(number, within, kind, rows):
        near[number, within, pl.ds(kind * SLAB, SLAB), :] = rows

    mine, theirs = [slab[...] for slab in slabs]
    project(place, counts, deltas, mine, theirs, wq, wkv, cos_ref, sin_ref, put)


def far_kernel(place, counts, *refs):
    slabs, (wq, wkv, cos_ref, sin_ref, first, near, queries, keyvals) = refs[:2], refs[2:]
    x = place[0]

    def put(number, within, kind, rows):
        owner = Z * ((x + 2) % X) + within
        if kind < HEADS:
            queries[owner, pl.ds(kind * SLAB, SLAB), :] = rows
        else:
            keyvals[owner, pl.ds((kind - HEADS) * SLAB, SLAB), :] = rows

    mine, theirs = [slab[...] for slab in slabs]
    project(place, counts, (2,), mine, theirs, wq, wkv, cos_ref, sin_ref, put)
    for piece, delta in ((first.at[0], 0), (near.at[0], 1), (near.at[1], 3)):
        for within in range(Z):
            owner = Z * ((x + delta) % X) + within
            queries[owner] = piece[within, :TILE]
            keyvals[owner] = piece[within, TILE:]


def newest_kernel(queries, keyvals, numer_ref, stat_ref):
    token = lax.broadcasted_iota(jnp.int32, (SLAB, TILE), 0)
    line = lax.broadcasted_iota(jnp.int32, (SLAB, TILE), 1) % SLAB
    seen = (line // STEPS == token // STEPS) & (token <= line)

    def some(step, carry):
        owners = [step * 8 + i for i in range(8)]
        scores = [
            lax.dot_general(
                keyvals[owner, :SLAB], queries[owner], (((1,), (1,)), ((), ())),
                preferred_element_type=jnp.float32,
            )
            for owner in owners
        ]
        mass = []
        for owner, score in zip(owners, scores):
            score = jnp.where(seen, score * (1.0 / math.sqrt(HEAD_SIZE)), -jnp.inf)
            peak = jnp.max(score, axis=0, keepdims=True)
            mass.append(jnp.exp(score - peak))
            stat_ref[owner, 0:1, :] = peak
            stat_ref[owner, 1:2, :] = jnp.sum(mass[-1], axis=0, keepdims=True)
        for owner, weights in zip(owners, mass):
            numer_ref[owner] = jnp.dot(
                weights.T.astype(jnp.bfloat16), keyvals[owner, SLAB:],
                preferred_element_type=jnp.float32,
            ).astype(jnp.bfloat16)
        return carry

    lax.fori_loop(0, OWNERS // 8, some, 0)


def prompt_kernel(tables, counts, queries, pages, answers):
    eye = diagonal()
    row = lax.broadcasted_iota(jnp.int32, (STAT_ROWS, HEAD_SIZE), 0)
    token = lax.broadcasted_iota(jnp.int32, (TILE, LONGEST_PAGES * PAGE_TOKENS), 1)
    scale = math.log2(math.e) / math.sqrt(HEAD_SIZE)

    def some(step, carry):
        groups = [step * 4 + i for i in range(4)]
        at = [[tables[g * LONGEST_PAGES + page] for page in range(LONGEST_PAGES)] for g in groups]
        scores = []
        for i, g in enumerate(groups):
            keys = jnp.concatenate([pages[p, 0] for p in at[i]], axis=0)
            scores.append(
                lax.dot_general(
                    queries[g], keys, (((1,), (1,)), ((), ())), preferred_element_type=jnp.float32
                )
            )
        mass, total, logs = [], [], []
        for g, score in zip(groups, scores):
            score = jnp.where(token < counts[g] * PAGE_TOKENS, score, -jnp.inf)
            peak = jnp.max(score, axis=-1, keepdims=True)
            mass.append(jnp.exp2((score - peak) * scale))
            total.append(jnp.sum(mass[-1], axis=-1, keepdims=True))
            logs.append(peak * (1.0 / math.sqrt(HEAD_SIZE)) + jnp.log(total[-1]))
        for i, g in enumerate(groups):
            values = jnp.concatenate([pages[p, 1] for p in at[i]], axis=0)
            numer = jnp.dot(mass[i].astype(jnp.bfloat16), values, preferred_element_type=jnp.float32)
            answers[g, pl.ds(0, TILE), :] = (numer / total[i]).astype(jnp.bfloat16)
            flat = jnp.sum(jnp.where(eye, logs[i], 0.0), axis=0, keepdims=True)
            stats = jnp.zeros((STAT_ROWS, HEAD_SIZE), jnp.float32)
            for piece in range(3):
                rounded = flat.astype(jnp.bfloat16).astype(jnp.float32)
                stats = jnp.where(row == piece, rounded, stats)
                flat = flat - rounded
            answers[g, pl.ds(TILE, STAT_ROWS), :] = stats.astype(jnp.bfloat16)
        return carry

    lax.fori_loop(0, OWNERS // 4, some, 0)


def merge_kernel(back, numer_ref, stat_ref, out):
    eye = diagonal()

    def some(step, carry):
        for i in range(4):
            owner = step * 4 + i
            stats = back[owner, pl.ds(TILE, STAT_ROWS), :].astype(jnp.float32)
            log_p = stats[0:1] + (stats[1:2] + stats[2:3])
            peak_n, total_n = stat_ref[owner, 0:1, :], stat_ref[owner, 1:2, :]
            log_n = peak_n + jnp.log(total_n)
            top = jnp.maximum(log_p, log_n)
            first, second = jnp.exp(log_p - top), jnp.exp(log_n - top)
            share_p = first / (first + second)
            share_n = second / ((first + second) * total_n)
            share_p = jnp.sum(jnp.where(eye, share_p, 0.0), axis=1, keepdims=True)
            share_n = jnp.sum(jnp.where(eye, share_n, 0.0), axis=1, keepdims=True)
            prompt = back[owner, pl.ds(0, TILE), :].astype(jnp.float32)
            newest = numer_ref[owner].astype(jnp.float32)
            merged = (prompt * share_p + newest * share_n).astype(jnp.bfloat16)
            for j in range(HEADS):
                out[owner, :, pl.ds(j * HEAD_SIZE, HEAD_SIZE)] = merged[j * SLAB:(j + 1) * SLAB]
        return carry

    lax.fori_loop(0, OWNERS // 4, some, 0)


def diagonal():
    first = lax.broadcasted_iota(jnp.int32, (TILE, HEAD_SIZE), 0)
    return first == lax.broadcasted_iota(jnp.int32, (TILE, HEAD_SIZE), 1)


VMEM = pl.BlockSpec(memory_space=pltpu.VMEM)
SMEM = pl.BlockSpec(memory_space=pltpu.SMEM)
ANY = pl.BlockSpec(memory_space=pl.ANY)


def params(mib):
    return pltpu.CompilerParams(vmem_limit_bytes=mib * MiB)


def body(
    new_states,
    w_query,
    keyvalue_weight,
    keyvalue_pages,
    page_table,
    prompt_pages,
    share_prompt,
    share_group,
):
    groups = lax.axis_size("dp")
    width = new_states.shape[2]
    tensor = lax.axis_index("tensor")
    place = jnp.stack([tensor // C, tensor % C]).astype(jnp.int32)

    targets = jnp.arange(groups, dtype=jnp.int32)
    match = (share_group[0][:, None] == targets[None, :]).astype(jnp.int32)
    dest_prompt = jnp.sum(match * share_prompt[0][:, None], axis=0)
    choose = (
        dest_prompt[:, None] == jnp.arange(prompt_pages.shape[1], dtype=jnp.int32)[None, :]
    ).astype(jnp.int32)
    dest_count = jnp.sum(choose * prompt_pages[0][None, :], axis=1)
    logical = (
        dest_prompt[:, None] * LONGEST_PAGES + jnp.arange(LONGEST_PAGES, dtype=jnp.int32)[None, :]
    )
    lookup = (
        logical[:, :, None] == jnp.arange(page_table.shape[1], dtype=jnp.int32)[None, None, :]
    ).astype(jnp.int32)
    physical = jnp.sum(lookup * page_table[0][None, None, :], axis=2).reshape(-1)
    slot_count = lax.all_to_all(dest_count, "dp", split_axis=0, concat_axis=0, tiled=True)
    cosine, sine = rope_tables()
    wkv = keyvalue_weight.reshape(width, -1)

    rows = new_states.shape[0] * STEPS
    own = pl.pallas_call(
        norm_kernel,
        out_shape=jax.ShapeDtypeStruct((rows, width), jnp.bfloat16),
        in_specs=[ANY],
        out_specs=VMEM,
        scratch_shapes=[
            pltpu.VMEM(new_states.shape, jnp.bfloat16),
            pltpu.VMEM((rows, width), jnp.float32),
            pltpu.SemaphoreType.DMA,
        ],
        compiler_params=params(8),
        name="norm",
    )(new_states)
    ahead = lax.ppermute(own, "tensor", along_x(1))
    behind = lax.ppermute(own, "tensor", along_x(-1))
    own_theirs = lax.ppermute(own, "tensor", other_core())

    def project_near(deltas, *slabs):
        return pl.pallas_call(
            functools.partial(near_kernel, deltas),
            out_shape=jax.ShapeDtypeStruct(
                (len(deltas), Z, TILE + 2 * SLAB, HEAD_SIZE), jnp.bfloat16
            ),
            in_specs=[SMEM] * 2 + [VMEM] * (len(slabs) + 4),
            out_specs=VMEM,
            compiler_params=params(16),
            name="project_near",
        )(place, slot_count, *slabs, w_query, wkv, cosine, sine)

    first = project_near((0,), own, own_theirs)
    half = jax.ShapeDtypeStruct((rows // 2, width), jnp.bfloat16)
    both, far_0, far_1 = pl.pallas_call(
        forward_kernel,
        out_shape=(jax.ShapeDtypeStruct((2 * rows, width), jnp.bfloat16), half, half),
        in_specs=[VMEM] * 3,
        out_specs=(VMEM,) * 3,
        compiler_params=params(4),
        name="forward",
    )(ahead, behind, first)
    far_0 = lax.ppermute(far_0, "tensor", along_x(1))
    far_1 = lax.ppermute(far_1, "tensor", along_x(-1))
    both_theirs = lax.ppermute(both, "tensor", other_core())
    near = project_near((1, 3), both, both_theirs)

    far = pl.pallas_call(
        join_kernel,
        out_shape=jax.ShapeDtypeStruct((rows, width), jnp.bfloat16),
        in_specs=[VMEM] * 3,
        out_specs=VMEM,
        compiler_params=params(4),
        name="join",
    )(far_0, far_1, near)
    far_theirs = lax.ppermute(far, "tensor", other_core())
    queries, keyvals = pl.pallas_call(
        far_kernel,
        out_shape=(
            jax.ShapeDtypeStruct((OWNERS, TILE, HEAD_SIZE), jnp.bfloat16),
            jax.ShapeDtypeStruct((OWNERS, 2 * SLAB, HEAD_SIZE), jnp.bfloat16),
        ),
        in_specs=[SMEM] * 2 + [VMEM] * 8,
        out_specs=(VMEM,) * 2,
        compiler_params=params(12),
        name="project_far",
    )(place, slot_count, far, far_theirs, w_query, wkv, cosine, sine, first, near)

    asked = lax.all_to_all(queries, "dp", split_axis=0, concat_axis=0, tiled=True)
    newest = pl.pallas_call(
        newest_kernel,
        out_shape=(
            jax.ShapeDtypeStruct((OWNERS, TILE, HEAD_SIZE), jnp.bfloat16),
            jax.ShapeDtypeStruct((OWNERS, 8, TILE), jnp.float32),
        ),
        in_specs=[VMEM] * 2,
        out_specs=(VMEM,) * 2,
        compiler_params=params(8),
        name="newest_tokens",
    )(queries, keyvals)
    answers = pl.pallas_call(
        prompt_kernel,
        out_shape=jax.ShapeDtypeStruct((OWNERS, TILE + STAT_ROWS, HEAD_SIZE), jnp.bfloat16),
        in_specs=[SMEM] * 2 + [VMEM] * 2,
        out_specs=VMEM,
        compiler_params=params(8),
        name="prompt_attention",
    )(physical, dest_count, asked, keyvalue_pages)
    back = lax.all_to_all(answers, "dp", split_axis=0, concat_axis=0, tiled=True)
    out = pl.pallas_call(
        merge_kernel,
        out_shape=jax.ShapeDtypeStruct((OWNERS, SLAB, HEADS * HEAD_SIZE), jnp.bfloat16),
        in_specs=[VMEM] * 3,
        out_specs=VMEM,
        compiler_params=params(8),
        name="merge",
    )(back, *newest)
    return out.reshape(groups * PROMPT_SAMPLES, STEPS, HEADS * HEAD_SIZE)


def solution(mesh):
    placed = (
        P(("dp", "tensor"), None, None),
        P(None, "tensor"),
        P(None, "tensor", None),
        P("dp", "tensor", None, None),
        P("dp", None),
        P("dp", None),
        P("dp", None),
        P("dp", None),
    )
    return jax.shard_map(
        body, mesh=mesh, in_specs=placed, out_specs=P("dp", None, "tensor"), check_vma=False
    )
```

```python
import functools
import math

import jax
import jax.numpy as jnp
from jax import lax
from jax.experimental import pallas as pl
from jax.experimental.pallas import tpu as pltpu
from jax.sharding import PartitionSpec as P

HEAD_SIZE = 128
PAGE_TOKENS = 128
LONGEST_PAGES = 4
PROMPT_SAMPLES = 8
STEPS = 4
EPSILON = 1e-06

Y, Z, X, C = 4, 8, 4, 2
SLAB = PROMPT_SAMPLES * STEPS
OWNERS = 32
HEADS = 4
TILE = HEADS * SLAB
STAT_ROWS = 8
MiB = 1024 * 1024


def along_x(step):
    return [(x * C + c, (x + step) % X * C + c) for x in range(X) for c in range(C)]


def other_core():
    return [(i, i ^ 1) for i in range(X * C)]


def rope_tables():
    half = HEAD_SIZE // 2
    freqs = jnp.exp(
        -(2.0 * jnp.arange(half, dtype=jnp.float32) / HEAD_SIZE) * jnp.log(1000000.0)
    )
    pages = jnp.arange(1, LONGEST_PAGES + 1, dtype=jnp.int32)[:, None]
    steps = jnp.arange(2 * STEPS, dtype=jnp.int32)[None, :] % STEPS
    angles = (PAGE_TOKENS * pages + steps).astype(jnp.float32)[..., None] * freqs
    cosine, sine = jnp.cos(angles), jnp.sin(angles)
    return (
        jnp.concatenate([cosine, cosine], axis=-1),
        jnp.concatenate([-sine, sine], axis=-1),
    )


def rotated(values, cosine, sine):
    values = values * lax.rsqrt(jnp.mean(values * values, axis=-1, keepdims=True) + EPSILON)
    turned = pltpu.roll(values, HEAD_SIZE // 2, 1)
    fold = (SLAB // 8, 8, HEAD_SIZE)
    out = values.reshape(fold) * cosine[None] + turned.reshape(fold) * sine[None]
    return out.reshape(SLAB, HEAD_SIZE)


def norm_kernel(states, slab, held, scratch, sem):
    load = pltpu.make_async_copy(states, held, sem)
    load.start()
    load.wait()
    for r in range(states.shape[0]):
        flat = held[r].astype(jnp.float32)
        flat = flat * lax.rsqrt(jnp.mean(flat * flat, axis=-1, keepdims=True) + EPSILON)
        scratch[r * STEPS:(r + 1) * STEPS, :] = flat
    slab[...] = scratch[...].astype(jnp.bfloat16)


def forward_kernel(ahead, behind, *refs):
    both, far_0, far_1 = refs[-3:]
    half = ahead.shape[0] // 2
    both[:2 * half] = behind[...]
    both[2 * half:] = ahead[...]
    far_0[...] = ahead[:half]
    far_1[...] = behind[half:]


def join_kernel(far_0, far_1, after, far):
    half = far_0.shape[0]
    far[:half] = far_0[...]
    far[half:] = far_1[...]


def project(place, counts, deltas, mine, theirs, wq, wkv, cos_ref, sin_ref, put):
    x, c = place[0], place[1]
    states = jnp.concatenate([mine, theirs], axis=0)
    slots = []
    for side in range(2):
        for number, delta in enumerate(deltas):
            for j in range(4):
                within = 4 * (c ^ side) + j
                n = counts[Z * ((x + delta) % X) + within]
                slots.append((number, within, cos_ref[n - 1], sin_ref[n - 1]))
    for block in range(3):
        weight = wq[:, block * 256:block * 256 + 256] if block < 2 else wkv[...]
        raw = jnp.dot(states, weight, preferred_element_type=jnp.float32)
        for slot, (number, within, cosine, sine) in enumerate(slots):
            rows = raw[slot * SLAB:(slot + 1) * SLAB]
            first, second = rows[:, :HEAD_SIZE], rows[:, HEAD_SIZE:]
            first = rotated(first, cosine, sine).astype(jnp.bfloat16)
            if block < 2:
                second = rotated(second, cosine, sine)
            second = second.astype(jnp.bfloat16)
            put(number, within, 2 * block, first)
            put(number, within, 2 * block + 1, second)


def near_kernel(deltas, place, counts, *refs):
    slabs, (wq, wkv, cos_ref, sin_ref, near) = refs[:-5], refs[-5:]

    def put(number, within, kind, rows):
        near[number, within, pl.ds(kind * SLAB, SLAB), :] = rows

    mine, theirs = [slab[...] for slab in slabs]
    project(place, counts, deltas, mine, theirs, wq, wkv, cos_ref, sin_ref, put)


def far_kernel(place, counts, *refs):
    slabs, (wq, wkv, cos_ref, sin_ref, first, near, queries, keyvals) = refs[:2], refs[2:]
    x = place[0]

    def put(number, within, kind, rows):
        owner = Z * ((x + 2) % X) + within
        if kind < HEADS:
            queries[owner, pl.ds(kind * SLAB, SLAB), :] = rows
        else:
            keyvals[owner, pl.ds((kind - HEADS) * SLAB, SLAB), :] = rows

    mine, theirs = [slab[...] for slab in slabs]
    project(place, counts, (2,), mine, theirs, wq, wkv, cos_ref, sin_ref, put)
    for piece, delta in ((first.at[0], 0), (near.at[0], 1), (near.at[1], 3)):
        for within in range(Z):
            owner = Z * ((x + delta) % X) + within
            queries[owner] = piece[within, :TILE]
            keyvals[owner] = piece[within, TILE:]


def newest_kernel(queries, keyvals, numer_ref, stat_ref):
    token = lax.broadcasted_iota(jnp.int32, (SLAB, TILE), 0)
    line = lax.broadcasted_iota(jnp.int32, (SLAB, TILE), 1) % SLAB
    seen = (line // STEPS == token // STEPS) & (token <= line)

    def some(step, carry):
        owners = [step * 8 + i for i in range(8)]
        scores = [
            lax.dot_general(
                keyvals[owner, :SLAB], queries[owner], (((1,), (1,)), ((), ())),
                preferred_element_type=jnp.float32,
            )
            for owner in owners
        ]
        mass = []
        for owner, score in zip(owners, scores):
            score = jnp.where(seen, score * (1.0 / math.sqrt(HEAD_SIZE)), -jnp.inf)
            peak = jnp.max(score, axis=0, keepdims=True)
            mass.append(jnp.exp(score - peak))
            stat_ref[owner, 0:1, :] = peak
            stat_ref[owner, 1:2, :] = jnp.sum(mass[-1], axis=0, keepdims=True)
        for owner, weights in zip(owners, mass):
            numer_ref[owner] = jnp.dot(
                weights.T.astype(jnp.bfloat16), keyvals[owner, SLAB:],
                preferred_element_type=jnp.float32,
            ).astype(jnp.bfloat16)
        return carry

    lax.fori_loop(0, OWNERS // 8, some, 0)


def prompt_kernel(tables, counts, queries, pages, answers):
    eye = diagonal()
    row = lax.broadcasted_iota(jnp.int32, (STAT_ROWS, HEAD_SIZE), 0)
    token = lax.broadcasted_iota(jnp.int32, (TILE, LONGEST_PAGES * PAGE_TOKENS), 1)
    scale = math.log2(math.e) / math.sqrt(HEAD_SIZE)

    def some(step, carry):
        groups = [step * 16 + i for i in range(16)]
        at = [[tables[g * LONGEST_PAGES + page] for page in range(LONGEST_PAGES)] for g in groups]
        scores = []
        for i, g in enumerate(groups):
            keys = jnp.concatenate([pages[p, 0] for p in at[i]], axis=0)
            scores.append(
                lax.dot_general(
                    queries[g], keys, (((1,), (1,)), ((), ())), preferred_element_type=jnp.float32
                )
            )
        mass, total, logs = [], [], []
        for g, score in zip(groups, scores):
            score = jnp.where(token < counts[g] * PAGE_TOKENS, score, -jnp.inf)
            peak = jnp.max(score, axis=-1, keepdims=True)
            mass.append(jnp.exp2((score - peak) * scale))
            total.append(jnp.sum(mass[-1], axis=-1, keepdims=True))
            logs.append(peak * (1.0 / math.sqrt(HEAD_SIZE)) + jnp.log(total[-1]))
        for i, g in enumerate(groups):
            values = jnp.concatenate([pages[p, 1] for p in at[i]], axis=0)
            numer = jnp.dot(mass[i].astype(jnp.bfloat16), values, preferred_element_type=jnp.float32)
            numer = numer / total[i]
            flat = jnp.sum(jnp.where(eye, logs[i], 0.0), axis=0, keepdims=True)
            stats = jnp.zeros((STAT_ROWS, HEAD_SIZE), jnp.float32)
            for piece in range(3):
                rounded = flat.astype(jnp.bfloat16).astype(jnp.float32)
                stats = jnp.where(row == piece, rounded, stats)
                flat = flat - rounded
            answers[g] = jnp.concatenate([numer, stats], axis=0).astype(jnp.bfloat16)
        return carry

    lax.fori_loop(0, OWNERS // 16, some, 0)


def merge_kernel(back, numer_ref, stat_ref, out):
    eye = diagonal()

    def some(step, carry):
        for i in range(4):
            owner = step * 4 + i
            message = back[owner].astype(jnp.float32)
            stats = message[TILE:]
            log_p = stats[0:1] + (stats[1:2] + stats[2:3])
            peak_n, total_n = stat_ref[owner, 0:1, :], stat_ref[owner, 1:2, :]
            log_n = peak_n + jnp.log(total_n)
            top = jnp.maximum(log_p, log_n)
            first, second = jnp.exp(log_p - top), jnp.exp(log_n - top)
            share_p = first / (first + second)
            share_n = second / ((first + second) * total_n)
            share_p = jnp.sum(jnp.where(eye, share_p, 0.0), axis=1, keepdims=True)
            share_n = jnp.sum(jnp.where(eye, share_n, 0.0), axis=1, keepdims=True)
            prompt = message[:TILE]
            newest = numer_ref[owner].astype(jnp.float32)
            merged = (prompt * share_p + newest * share_n)
            for j in range(HEADS):
                rows = merged[j * SLAB:(j + 1) * SLAB].reshape(PROMPT_SAMPLES, STEPS, HEAD_SIZE)
                samples = pl.ds(owner * PROMPT_SAMPLES, PROMPT_SAMPLES)
                out[samples, :, pl.ds(j * HEAD_SIZE, HEAD_SIZE)] = rows.astype(jnp.bfloat16)
        return carry

    lax.fori_loop(0, OWNERS // 4, some, 0)


def diagonal():
    first = lax.broadcasted_iota(jnp.int32, (TILE, HEAD_SIZE), 0)
    return first == lax.broadcasted_iota(jnp.int32, (TILE, HEAD_SIZE), 1)


VMEM = pl.BlockSpec(memory_space=pltpu.VMEM)
SMEM = pl.BlockSpec(memory_space=pltpu.SMEM)
ANY = pl.BlockSpec(memory_space=pl.ANY)


def params(mib):
    return pltpu.CompilerParams(vmem_limit_bytes=mib * MiB)


def body(
    new_states,
    w_query,
    keyvalue_weight,
    keyvalue_pages,
    page_table,
    prompt_pages,
    share_prompt,
    share_group,
):
    groups = lax.axis_size("dp")
    width = new_states.shape[2]
    tensor = lax.axis_index("tensor")
    place = jnp.stack([tensor // C, tensor % C]).astype(jnp.int32)

    targets = jnp.arange(groups, dtype=jnp.int32)
    match = (share_group[0][:, None] == targets[None, :]).astype(jnp.int32)
    dest_prompt = jnp.sum(match * share_prompt[0][:, None], axis=0)
    choose = (
        dest_prompt[:, None] == jnp.arange(prompt_pages.shape[1], dtype=jnp.int32)[None, :]
    ).astype(jnp.int32)
    dest_count = jnp.sum(choose * prompt_pages[0][None, :], axis=1)
    logical = (
        dest_prompt[:, None] * LONGEST_PAGES + jnp.arange(LONGEST_PAGES, dtype=jnp.int32)[None, :]
    )
    lookup = (
        logical[:, :, None] == jnp.arange(page_table.shape[1], dtype=jnp.int32)[None, None, :]
    ).astype(jnp.int32)
    physical = jnp.sum(lookup * page_table[0][None, None, :], axis=2).reshape(-1)
    slot_count = lax.all_to_all(dest_count, "dp", split_axis=0, concat_axis=0, tiled=True)
    cosine, sine = rope_tables()
    wkv = keyvalue_weight.reshape(width, -1)

    rows = new_states.shape[0] * STEPS
    own = pl.pallas_call(
        norm_kernel,
        out_shape=jax.ShapeDtypeStruct((rows, width), jnp.bfloat16),
        in_specs=[ANY],
        out_specs=VMEM,
        scratch_shapes=[
            pltpu.VMEM(new_states.shape, jnp.bfloat16),
            pltpu.VMEM((rows, width), jnp.float32),
            pltpu.SemaphoreType.DMA,
        ],
        compiler_params=params(8),
        name="norm",
    )(new_states)
    ahead = lax.ppermute(own, "tensor", along_x(1))
    behind = lax.ppermute(own, "tensor", along_x(-1))
    own_theirs = lax.ppermute(own, "tensor", other_core())

    def project_near(deltas, *slabs):
        return pl.pallas_call(
            functools.partial(near_kernel, deltas),
            out_shape=jax.ShapeDtypeStruct(
                (len(deltas), Z, TILE + 2 * SLAB, HEAD_SIZE), jnp.bfloat16
            ),
            in_specs=[SMEM] * 2 + [VMEM] * (len(slabs) + 4),
            out_specs=VMEM,
            compiler_params=params(16),
            name="project_near",
        )(place, slot_count, *slabs, w_query, wkv, cosine, sine)

    first = project_near((0,), own, own_theirs)
    half = jax.ShapeDtypeStruct((rows // 2, width), jnp.bfloat16)
    both, far_0, far_1 = pl.pallas_call(
        forward_kernel,
        out_shape=(jax.ShapeDtypeStruct((2 * rows, width), jnp.bfloat16), half, half),
        in_specs=[VMEM] * 3,
        out_specs=(VMEM,) * 3,
        compiler_params=params(4),
        name="forward",
    )(ahead, behind, first)
    far_0 = lax.ppermute(far_0, "tensor", along_x(1))
    far_1 = lax.ppermute(far_1, "tensor", along_x(-1))
    both_theirs = lax.ppermute(both, "tensor", other_core())
    near = project_near((1, 3), both, both_theirs)

    far = pl.pallas_call(
        join_kernel,
        out_shape=jax.ShapeDtypeStruct((rows, width), jnp.bfloat16),
        in_specs=[VMEM] * 3,
        out_specs=VMEM,
        compiler_params=params(4),
        name="join",
    )(far_0, far_1, near)
    far_theirs = lax.ppermute(far, "tensor", other_core())
    queries, keyvals = pl.pallas_call(
        far_kernel,
        out_shape=(
            jax.ShapeDtypeStruct((OWNERS, TILE, HEAD_SIZE), jnp.bfloat16),
            jax.ShapeDtypeStruct((OWNERS, 2 * SLAB, HEAD_SIZE), jnp.bfloat16),
        ),
        in_specs=[SMEM] * 2 + [VMEM] * 8,
        out_specs=(VMEM,) * 2,
        compiler_params=params(12),
        name="project_far",
    )(place, slot_count, far, far_theirs, w_query, wkv, cosine, sine, first, near)

    asked = lax.all_to_all(queries, "dp", split_axis=0, concat_axis=0, tiled=True)
    newest = pl.pallas_call(
        newest_kernel,
        out_shape=(
            jax.ShapeDtypeStruct((OWNERS, TILE, HEAD_SIZE), jnp.bfloat16),
            jax.ShapeDtypeStruct((OWNERS, 8, TILE), jnp.float32),
        ),
        in_specs=[VMEM] * 2,
        out_specs=(VMEM,) * 2,
        compiler_params=params(8),
        name="newest_tokens",
    )(queries, keyvals)
    answers = pl.pallas_call(
        prompt_kernel,
        out_shape=jax.ShapeDtypeStruct((OWNERS, TILE + STAT_ROWS, HEAD_SIZE), jnp.bfloat16),
        in_specs=[SMEM] * 2 + [VMEM] * 2,
        out_specs=VMEM,
        compiler_params=params(8),
        name="prompt_attention",
    )(physical, dest_count, asked, keyvalue_pages)
    back = lax.all_to_all(answers, "dp", split_axis=0, concat_axis=0, tiled=True)
    return pl.pallas_call(
        merge_kernel,
        out_shape=jax.ShapeDtypeStruct(
            (groups * PROMPT_SAMPLES, STEPS, HEADS * HEAD_SIZE), jnp.bfloat16
        ),
        in_specs=[VMEM] * 3,
        out_specs=VMEM,
        compiler_params=params(8),
        name="merge",
    )(back, *newest)


def solution(mesh):
    placed = (
        P(("dp", "tensor"), None, None),
        P(None, "tensor"),
        P(None, "tensor", None),
        P("dp", "tensor", None, None),
        P("dp", None),
        P("dp", None),
        P("dp", None),
        P("dp", None),
    )
    return jax.shard_map(
        body, mesh=mesh, in_specs=placed, out_specs=P("dp", None, "tensor"), check_vma=False
    )
```

```python
import functools
import math

import jax
import jax.numpy as jnp
from jax import lax
from jax.experimental import pallas as pl
from jax.experimental.pallas import tpu as pltpu
from jax.sharding import PartitionSpec as P

HEAD_SIZE = 128
PAGE_TOKENS = 128
LONGEST_PAGES = 4
PROMPT_SAMPLES = 8
STEPS = 4
EPSILON = 1e-06

Y, Z, X, C = 4, 8, 4, 2
SLAB = PROMPT_SAMPLES * STEPS
OWNERS = 32
HEADS = 4
TILE = HEADS * SLAB
STAT_ROWS = 8
MiB = 1024 * 1024


def along_x(step):
    return [(x * C + c, (x + step) % X * C + c) for x in range(X) for c in range(C)]


def other_core():
    return [(i, i ^ 1) for i in range(X * C)]


def rope_tables():
    half = HEAD_SIZE // 2
    freqs = jnp.exp(
        -(2.0 * jnp.arange(half, dtype=jnp.float32) / HEAD_SIZE) * jnp.log(1000000.0)
    )
    pages = jnp.arange(1, LONGEST_PAGES + 1, dtype=jnp.int32)[:, None]
    steps = jnp.arange(2 * STEPS, dtype=jnp.int32)[None, :] % STEPS
    angles = (PAGE_TOKENS * pages + steps).astype(jnp.float32)[..., None] * freqs
    cosine, sine = jnp.cos(angles), jnp.sin(angles)
    return (
        jnp.concatenate([cosine, cosine], axis=-1),
        jnp.concatenate([-sine, sine], axis=-1),
    )


def rotated(values, cosine, sine):
    values = values * lax.rsqrt(jnp.mean(values * values, axis=-1, keepdims=True) + EPSILON)
    turned = pltpu.roll(values, HEAD_SIZE // 2, 1)
    fold = (SLAB // 8, 8, HEAD_SIZE)
    out = values.reshape(fold) * cosine[None] + turned.reshape(fold) * sine[None]
    return out.reshape(SLAB, HEAD_SIZE)


def norm_kernel(states, slab, held, scratch, sem):
    load = pltpu.make_async_copy(states, held, sem)
    load.start()
    load.wait()
    for r in range(states.shape[0]):
        flat = held[r].astype(jnp.float32)
        flat = flat * lax.rsqrt(jnp.mean(flat * flat, axis=-1, keepdims=True) + EPSILON)
        scratch[r * STEPS:(r + 1) * STEPS, :] = flat
    slab[...] = scratch[...].astype(jnp.bfloat16)


def forward_kernel(ahead, behind, *refs):
    both, far_0, far_1 = refs[-3:]
    half = ahead.shape[0] // 2
    both[:2 * half] = behind[...]
    both[2 * half:] = ahead[...]
    far_0[...] = ahead[:half]
    far_1[...] = behind[half:]


def join_kernel(far_0, far_1, after, far):
    half = far_0.shape[0]
    far[:half] = far_0[...]
    far[half:] = far_1[...]


def project(place, counts, deltas, mine, theirs, wq, wkv, cos_ref, sin_ref, put):
    x, c = place[0], place[1]
    states = jnp.concatenate([mine, theirs], axis=0)
    slots = []
    for side in range(2):
        for number, delta in enumerate(deltas):
            for j in range(4):
                within = 4 * (c ^ side) + j
                n = counts[Z * ((x + delta) % X) + within]
                slots.append((number, within, cos_ref[n - 1], sin_ref[n - 1]))
    for block in range(3):
        weight = wq[:, block * 256:block * 256 + 256] if block < 2 else wkv[...]
        raw = jnp.dot(states, weight, preferred_element_type=jnp.float32)
        for slot, (number, within, cosine, sine) in enumerate(slots):
            rows = raw[slot * SLAB:(slot + 1) * SLAB]
            first, second = rows[:, :HEAD_SIZE], rows[:, HEAD_SIZE:]
            first = rotated(first, cosine, sine).astype(jnp.bfloat16)
            if block < 2:
                second = rotated(second, cosine, sine)
            second = second.astype(jnp.bfloat16)
            put(number, within, 2 * block, first)
            put(number, within, 2 * block + 1, second)


def near_kernel(deltas, place, counts, *refs):
    slabs, (wq, wkv, cos_ref, sin_ref, near) = refs[:-5], refs[-5:]

    def put(number, within, kind, rows):
        near[number, within, pl.ds(kind * SLAB, SLAB), :] = rows

    mine, theirs = [slab[...] for slab in slabs]
    project(place, counts, deltas, mine, theirs, wq, wkv, cos_ref, sin_ref, put)


def far_kernel(place, counts, *refs):
    slabs, (wq, wkv, cos_ref, sin_ref, first, near, queries, keyvals) = refs[:2], refs[2:]
    x = place[0]

    def put(number, within, kind, rows):
        owner = Z * ((x + 2) % X) + within
        if kind < HEADS:
            queries[owner, pl.ds(kind * SLAB, SLAB), :] = rows
        else:
            keyvals[owner, pl.ds((kind - HEADS) * SLAB, SLAB), :] = rows

    mine, theirs = [slab[...] for slab in slabs]
    project(place, counts, (2,), mine, theirs, wq, wkv, cos_ref, sin_ref, put)
    for piece, delta in ((first.at[0], 0), (near.at[0], 1), (near.at[1], 3)):
        for within in range(Z):
            owner = Z * ((x + delta) % X) + within
            queries[owner] = piece[within, :TILE]
            keyvals[owner] = piece[within, TILE:]


def newest_kernel(queries, keyvals, numer_ref, stat_ref):
    token = lax.broadcasted_iota(jnp.int32, (SLAB, TILE), 0)
    line = lax.broadcasted_iota(jnp.int32, (SLAB, TILE), 1) % SLAB
    seen = (line // STEPS == token // STEPS) & (token <= line)

    def some(step, carry):
        owners = [step * 8 + i for i in range(8)]
        scores = [
            lax.dot_general(
                keyvals[owner, :SLAB], queries[owner], (((1,), (1,)), ((), ())),
                preferred_element_type=jnp.float32,
            )
            for owner in owners
        ]
        mass = []
        for owner, score in zip(owners, scores):
            score = jnp.where(seen, score * (1.0 / math.sqrt(HEAD_SIZE)), -jnp.inf)
            peak = jnp.max(score, axis=0, keepdims=True)
            mass.append(jnp.exp(score - peak))
            stat_ref[owner, 0:1, :] = peak
            stat_ref[owner, 1:2, :] = jnp.sum(mass[-1], axis=0, keepdims=True)
        for owner, weights in zip(owners, mass):
            numer_ref[owner] = jnp.dot(
                weights.T.astype(jnp.bfloat16), keyvals[owner, SLAB:],
                preferred_element_type=jnp.float32,
            ).astype(jnp.bfloat16)
        return carry

    lax.fori_loop(0, OWNERS // 8, some, 0)


def prompt_kernel(tables, counts, queries, pages, after, answers):
    eye = diagonal()
    row = lax.broadcasted_iota(jnp.int32, (STAT_ROWS, HEAD_SIZE), 0)
    token = lax.broadcasted_iota(jnp.int32, (TILE, LONGEST_PAGES * PAGE_TOKENS), 1)
    scale = math.log2(math.e) / math.sqrt(HEAD_SIZE)

    def some(step, carry):
        groups = [step * 16 + i for i in range(16)]
        at = [[tables[g * LONGEST_PAGES + page] for page in range(LONGEST_PAGES)] for g in groups]
        scores = []
        for i, g in enumerate(groups):
            keys = jnp.concatenate([pages[p, 0] for p in at[i]], axis=0)
            scores.append(
                lax.dot_general(
                    queries[g], keys, (((1,), (1,)), ((), ())), preferred_element_type=jnp.float32
                )
            )
        mass, total, logs = [], [], []
        for g, score in zip(groups, scores):
            score = jnp.where(token < counts[g] * PAGE_TOKENS, score, -jnp.inf)
            peak = jnp.max(score, axis=-1, keepdims=True)
            mass.append(jnp.exp2((score - peak) * scale))
            total.append(jnp.sum(mass[-1], axis=-1, keepdims=True))
            logs.append(peak * (1.0 / math.sqrt(HEAD_SIZE)) + jnp.log(total[-1]))
        for i, g in enumerate(groups):
            values = jnp.concatenate([pages[p, 1] for p in at[i]], axis=0)
            numer = jnp.dot(mass[i].astype(jnp.bfloat16), values, preferred_element_type=jnp.float32)
            numer = numer / total[i]
            flat = jnp.sum(jnp.where(eye, logs[i], 0.0), axis=0, keepdims=True)
            stats = jnp.zeros((STAT_ROWS, HEAD_SIZE), jnp.float32)
            for piece in range(3):
                rounded = flat.astype(jnp.bfloat16).astype(jnp.float32)
                stats = jnp.where(row == piece, rounded, stats)
                flat = flat - rounded
            answers[g] = jnp.concatenate([numer, stats], axis=0).astype(jnp.bfloat16)
        return carry

    lax.fori_loop(0, OWNERS // 16, some, 0)


def merge_kernel(back, numer_ref, stat_ref, out):
    eye = diagonal()

    def some(step, carry):
        for i in range(16):
            owner = step * 16 + i
            message = back[owner].astype(jnp.float32)
            stats = message[TILE:]
            log_p = stats[0:1] + (stats[1:2] + stats[2:3])
            peak_n, total_n = stat_ref[owner, 0:1, :], stat_ref[owner, 1:2, :]
            log_n = peak_n + jnp.log(total_n)
            top = jnp.maximum(log_p, log_n)
            first, second = jnp.exp(log_p - top), jnp.exp(log_n - top)
            share_p = first / (first + second)
            share_n = second / ((first + second) * total_n)
            share_p = jnp.sum(jnp.where(eye, share_p, 0.0), axis=1, keepdims=True)
            share_n = jnp.sum(jnp.where(eye, share_n, 0.0), axis=1, keepdims=True)
            prompt = message[:TILE]
            newest = numer_ref[owner].astype(jnp.float32)
            merged = (prompt * share_p + newest * share_n)
            for j in range(HEADS):
                rows = merged[j * SLAB:(j + 1) * SLAB].reshape(PROMPT_SAMPLES, STEPS, HEAD_SIZE)
                samples = pl.ds(owner * PROMPT_SAMPLES, PROMPT_SAMPLES)
                out[samples, :, pl.ds(j * HEAD_SIZE, HEAD_SIZE)] = rows.astype(jnp.bfloat16)
        return carry

    lax.fori_loop(0, OWNERS // 16, some, 0)


def diagonal():
    first = lax.broadcasted_iota(jnp.int32, (TILE, HEAD_SIZE), 0)
    return first == lax.broadcasted_iota(jnp.int32, (TILE, HEAD_SIZE), 1)


VMEM = pl.BlockSpec(memory_space=pltpu.VMEM)
SMEM = pl.BlockSpec(memory_space=pltpu.SMEM)
ANY = pl.BlockSpec(memory_space=pl.ANY)


def params(mib):
    return pltpu.CompilerParams(vmem_limit_bytes=mib * MiB)


def body(
    new_states,
    w_query,
    keyvalue_weight,
    keyvalue_pages,
    page_table,
    prompt_pages,
    share_prompt,
    share_group,
):
    groups = lax.axis_size("dp")
    width = new_states.shape[2]
    tensor = lax.axis_index("tensor")
    place = jnp.stack([tensor // C, tensor % C]).astype(jnp.int32)

    targets = jnp.arange(groups, dtype=jnp.int32)
    match = (share_group[0][:, None] == targets[None, :]).astype(jnp.int32)
    dest_prompt = jnp.sum(match * share_prompt[0][:, None], axis=0)
    choose = (
        dest_prompt[:, None] == jnp.arange(prompt_pages.shape[1], dtype=jnp.int32)[None, :]
    ).astype(jnp.int32)
    dest_count = jnp.sum(choose * prompt_pages[0][None, :], axis=1)
    logical = (
        dest_prompt[:, None] * LONGEST_PAGES + jnp.arange(LONGEST_PAGES, dtype=jnp.int32)[None, :]
    )
    lookup = (
        logical[:, :, None] == jnp.arange(page_table.shape[1], dtype=jnp.int32)[None, None, :]
    ).astype(jnp.int32)
    physical = jnp.sum(lookup * page_table[0][None, None, :], axis=2).reshape(-1)
    slot_count = lax.all_to_all(dest_count, "dp", split_axis=0, concat_axis=0, tiled=True)
    cosine, sine = rope_tables()
    wkv = keyvalue_weight.reshape(width, -1)

    rows = new_states.shape[0] * STEPS
    own = pl.pallas_call(
        norm_kernel,
        out_shape=jax.ShapeDtypeStruct((rows, width), jnp.bfloat16),
        in_specs=[ANY],
        out_specs=VMEM,
        scratch_shapes=[
            pltpu.VMEM(new_states.shape, jnp.bfloat16),
            pltpu.VMEM((rows, width), jnp.float32),
            pltpu.SemaphoreType.DMA,
        ],
        compiler_params=params(8),
        name="norm",
    )(new_states)
    ahead = lax.ppermute(own, "tensor", along_x(1))
    behind = lax.ppermute(own, "tensor", along_x(-1))
    own_theirs = lax.ppermute(own, "tensor", other_core())

    def project_near(deltas, *slabs):
        return pl.pallas_call(
            functools.partial(near_kernel, deltas),
            out_shape=jax.ShapeDtypeStruct(
                (len(deltas), Z, TILE + 2 * SLAB, HEAD_SIZE), jnp.bfloat16
            ),
            in_specs=[SMEM] * 2 + [VMEM] * (len(slabs) + 4),
            out_specs=VMEM,
            compiler_params=params(16),
            name="project_near",
        )(place, slot_count, *slabs, w_query, wkv, cosine, sine)

    first = project_near((0,), own, own_theirs)
    half = jax.ShapeDtypeStruct((rows // 2, width), jnp.bfloat16)
    both, far_0, far_1 = pl.pallas_call(
        forward_kernel,
        out_shape=(jax.ShapeDtypeStruct((2 * rows, width), jnp.bfloat16), half, half),
        in_specs=[VMEM] * 3,
        out_specs=(VMEM,) * 3,
        compiler_params=params(4),
        name="forward",
    )(ahead, behind, first)
    far_0 = lax.ppermute(far_0, "tensor", along_x(1))
    far_1 = lax.ppermute(far_1, "tensor", along_x(-1))
    both_theirs = lax.ppermute(both, "tensor", other_core())
    near = project_near((1, 3), both, both_theirs)

    far = pl.pallas_call(
        join_kernel,
        out_shape=jax.ShapeDtypeStruct((rows, width), jnp.bfloat16),
        in_specs=[VMEM] * 3,
        out_specs=VMEM,
        compiler_params=params(4),
        name="join",
    )(far_0, far_1, near)
    far_theirs = lax.ppermute(far, "tensor", other_core())
    queries, keyvals = pl.pallas_call(
        far_kernel,
        out_shape=(
            jax.ShapeDtypeStruct((OWNERS, TILE, HEAD_SIZE), jnp.bfloat16),
            jax.ShapeDtypeStruct((OWNERS, 2 * SLAB, HEAD_SIZE), jnp.bfloat16),
        ),
        in_specs=[SMEM] * 2 + [VMEM] * 8,
        out_specs=(VMEM,) * 2,
        compiler_params=params(12),
        name="project_far",
    )(place, slot_count, far, far_theirs, w_query, wkv, cosine, sine, first, near)

    asked = lax.all_to_all(queries, "dp", split_axis=0, concat_axis=0, tiled=True)
    newest = pl.pallas_call(
        newest_kernel,
        out_shape=(
            jax.ShapeDtypeStruct((OWNERS, TILE, HEAD_SIZE), jnp.bfloat16),
            jax.ShapeDtypeStruct((OWNERS, 8, TILE), jnp.float32),
        ),
        in_specs=[VMEM] * 2,
        out_specs=(VMEM,) * 2,
        compiler_params=params(8),
        name="newest_tokens",
    )(queries, keyvals)
    answers = pl.pallas_call(
        prompt_kernel,
        out_shape=jax.ShapeDtypeStruct((OWNERS, TILE + STAT_ROWS, HEAD_SIZE), jnp.bfloat16),
        in_specs=[SMEM] * 2 + [VMEM] * 3,
        out_specs=VMEM,
        compiler_params=params(8),
        name="prompt_attention",
    )(physical, dest_count, asked, keyvalue_pages, newest[1])
    back = lax.all_to_all(answers, "dp", split_axis=0, concat_axis=0, tiled=True)
    return pl.pallas_call(
        merge_kernel,
        out_shape=jax.ShapeDtypeStruct(
            (groups * PROMPT_SAMPLES, STEPS, HEADS * HEAD_SIZE), jnp.bfloat16
        ),
        in_specs=[VMEM] * 3,
        out_specs=VMEM,
        compiler_params=params(8),
        name="merge",
    )(back, *newest)


def solution(mesh):
    placed = (
        P(("dp", "tensor"), None, None),
        P(None, "tensor"),
        P(None, "tensor", None),
        P("dp", "tensor", None, None),
        P("dp", None),
        P("dp", None),
        P("dp", None),
        P("dp", None),
    )
    return jax.shard_map(
        body, mesh=mesh, in_specs=placed, out_specs=P("dp", None, "tensor"), check_vma=False
    )
```

```python
import functools
import math

import jax
import jax.numpy as jnp
from jax import lax
from jax.experimental import pallas as pl
from jax.experimental.pallas import tpu as pltpu
from jax.sharding import PartitionSpec as P

HEAD_SIZE = 128
PAGE_TOKENS = 128
LONGEST_PAGES = 4
PROMPT_SAMPLES = 8
STEPS = 4
EPSILON = 1e-06

Y, Z, X, C = 4, 8, 4, 2
SLAB = PROMPT_SAMPLES * STEPS
OWNERS = 32
HEADS = 4
TILE = HEADS * SLAB
STAT_ROWS = 8
MiB = 1024 * 1024


def along_x(step):
    return [(x * C + c, (x + step) % X * C + c) for x in range(X) for c in range(C)]


def other_core():
    return [(i, i ^ 1) for i in range(X * C)]


def rope_tables():
    half = HEAD_SIZE // 2
    freqs = jnp.exp(
        -(2.0 * jnp.arange(half, dtype=jnp.float32) / HEAD_SIZE) * jnp.log(1000000.0)
    )
    pages = jnp.arange(1, LONGEST_PAGES + 1, dtype=jnp.int32)[:, None]
    steps = jnp.arange(2 * STEPS, dtype=jnp.int32)[None, :] % STEPS
    angles = (PAGE_TOKENS * pages + steps).astype(jnp.float32)[..., None] * freqs
    cosine, sine = jnp.cos(angles), jnp.sin(angles)
    return (
        jnp.concatenate([cosine, cosine], axis=-1),
        jnp.concatenate([-sine, sine], axis=-1),
    )


def rotated(values, cosine, sine):
    values = values * lax.rsqrt(jnp.mean(values * values, axis=-1, keepdims=True) + EPSILON)
    turned = pltpu.roll(values, HEAD_SIZE // 2, 1)
    fold = (SLAB // 8, 8, HEAD_SIZE)
    out = values.reshape(fold) * cosine[None] + turned.reshape(fold) * sine[None]
    return out.reshape(SLAB, HEAD_SIZE)


def norm_kernel(states, slab, scratch):
    for r in range(states.shape[0]):
        flat = states[r].astype(jnp.float32)
        flat = flat * lax.rsqrt(jnp.mean(flat * flat, axis=-1, keepdims=True) + EPSILON)
        scratch[r * STEPS:(r + 1) * STEPS, :] = flat
    slab[...] = scratch[...].astype(jnp.bfloat16)


def forward_kernel(ahead, behind, *refs):
    both, far_0, far_1 = refs[-3:]
    half = ahead.shape[0] // 2
    both[:2 * half] = behind[...]
    both[2 * half:] = ahead[...]
    far_0[...] = ahead[:half]
    far_1[...] = behind[half:]


def join_kernel(far_0, far_1, after, far):
    half = far_0.shape[0]
    far[:half] = far_0[...]
    far[half:] = far_1[...]


def project(place, counts, deltas, mine, theirs, wq, wkv, cos_ref, sin_ref, put):
    x, c = place[0], place[1]
    states = jnp.concatenate([mine, theirs], axis=0)
    slots = []
    for side in range(2):
        for number, delta in enumerate(deltas):
            for j in range(4):
                within = 4 * (c ^ side) + j
                n = counts[Z * ((x + delta) % X) + within]
                slots.append((number, within, cos_ref[n - 1], sin_ref[n - 1]))
    for block in range(3):
        weight = wq[:, block * 256:block * 256 + 256] if block < 2 else wkv[...]
        raw = jnp.dot(states, weight, preferred_element_type=jnp.float32)
        for slot, (number, within, cosine, sine) in enumerate(slots):
            rows = raw[slot * SLAB:(slot + 1) * SLAB]
            first, second = rows[:, :HEAD_SIZE], rows[:, HEAD_SIZE:]
            first = rotated(first, cosine, sine).astype(jnp.bfloat16)
            if block < 2:
                second = rotated(second, cosine, sine)
            second = second.astype(jnp.bfloat16)
            put(number, within, 2 * block, first)
            put(number, within, 2 * block + 1, second)


def near_kernel(deltas, place, counts, *refs):
    slabs, (wq, wkv, cos_ref, sin_ref, near) = refs[:-5], refs[-5:]

    def put(number, within, kind, rows):
        near[number, within, pl.ds(kind * SLAB, SLAB), :] = rows

    mine, theirs = [slab[...] for slab in slabs]
    project(place, counts, deltas, mine, theirs, wq, wkv, cos_ref, sin_ref, put)


def far_kernel(place, counts, *refs):
    slabs, (wq, wkv, cos_ref, sin_ref, first, near, queries, keyvals) = refs[:2], refs[2:]
    x = place[0]

    def put(number, within, kind, rows):
        owner = Z * ((x + 2) % X) + within
        if kind < HEADS:
            queries[owner, pl.ds(kind * SLAB, SLAB), :] = rows
        else:
            keyvals[owner, pl.ds((kind - HEADS) * SLAB, SLAB), :] = rows

    mine, theirs = [slab[...] for slab in slabs]
    project(place, counts, (2,), mine, theirs, wq, wkv, cos_ref, sin_ref, put)
    for piece, delta in ((first.at[0], 0), (near.at[0], 1), (near.at[1], 3)):
        for within in range(Z):
            owner = Z * ((x + delta) % X) + within
            queries[owner] = piece[within, :TILE]
            keyvals[owner] = piece[within, TILE:]


def newest_kernel(queries, keyvals, numer_ref, stat_ref):
    token = lax.broadcasted_iota(jnp.int32, (SLAB, TILE), 0)
    line = lax.broadcasted_iota(jnp.int32, (SLAB, TILE), 1) % SLAB
    seen = (line // STEPS == token // STEPS) & (token <= line)

    def some(step, carry):
        owners = [step * 8 + i for i in range(8)]
        scores = [
            lax.dot_general(
                keyvals[owner, :SLAB], queries[owner], (((1,), (1,)), ((), ())),
                preferred_element_type=jnp.float32,
            )
            for owner in owners
        ]
        mass = []
        for owner, score in zip(owners, scores):
            score = jnp.where(seen, score * (1.0 / math.sqrt(HEAD_SIZE)), -jnp.inf)
            peak = jnp.max(score, axis=0, keepdims=True)
            mass.append(jnp.exp(score - peak))
            stat_ref[owner, 0:1, :] = peak
            stat_ref[owner, 1:2, :] = jnp.sum(mass[-1], axis=0, keepdims=True)
        for owner, weights in zip(owners, mass):
            numer_ref[owner] = jnp.dot(
                weights.T.astype(jnp.bfloat16), keyvals[owner, SLAB:],
                preferred_element_type=jnp.float32,
            ).astype(jnp.bfloat16)
        return carry

    lax.fori_loop(0, OWNERS // 8, some, 0)


def prompt_kernel(tables, counts, queries, pages, after, answers):
    eye = diagonal()
    row = lax.broadcasted_iota(jnp.int32, (STAT_ROWS, HEAD_SIZE), 0)
    token = lax.broadcasted_iota(jnp.int32, (TILE, LONGEST_PAGES * PAGE_TOKENS), 1)
    scale = math.log2(math.e) / math.sqrt(HEAD_SIZE)

    def some(step, carry):
        groups = [step * 16 + i for i in range(16)]
        at = [[tables[g * LONGEST_PAGES + page] for page in range(LONGEST_PAGES)] for g in groups]
        scores = []
        for i, g in enumerate(groups):
            keys = jnp.concatenate([pages[p, 0] for p in at[i]], axis=0)
            scores.append(
                lax.dot_general(
                    queries[g], keys, (((1,), (1,)), ((), ())), preferred_element_type=jnp.float32
                )
            )
        mass, total, logs = [], [], []
        for g, score in zip(groups, scores):
            score = jnp.where(token < counts[g] * PAGE_TOKENS, score, -jnp.inf)
            peak = jnp.max(score, axis=-1, keepdims=True)
            mass.append(jnp.exp2((score - peak) * scale))
            total.append(jnp.sum(mass[-1], axis=-1, keepdims=True))
            logs.append(peak * (1.0 / math.sqrt(HEAD_SIZE)) + jnp.log(total[-1]))
        for i, g in enumerate(groups):
            values = jnp.concatenate([pages[p, 1] for p in at[i]], axis=0)
            numer = jnp.dot(mass[i].astype(jnp.bfloat16), values, preferred_element_type=jnp.float32)
            numer = numer / total[i]
            flat = jnp.sum(jnp.where(eye, logs[i], 0.0), axis=0, keepdims=True)
            stats = jnp.zeros((STAT_ROWS, HEAD_SIZE), jnp.float32)
            for piece in range(3):
                rounded = flat.astype(jnp.bfloat16).astype(jnp.float32)
                stats = jnp.where(row == piece, rounded, stats)
                flat = flat - rounded
            answers[g] = jnp.concatenate([numer, stats], axis=0).astype(jnp.bfloat16)
        return carry

    lax.fori_loop(0, OWNERS // 16, some, 0)


def merge_kernel(back, numer_ref, stat_ref, out):
    eye = diagonal()

    def some(step, carry):
        for i in range(16):
            owner = step * 16 + i
            message = back[owner].astype(jnp.float32)
            stats = message[TILE:]
            log_p = stats[0:1] + (stats[1:2] + stats[2:3])
            peak_n, total_n = stat_ref[owner, 0:1, :], stat_ref[owner, 1:2, :]
            log_n = peak_n + jnp.log(total_n)
            top = jnp.maximum(log_p, log_n)
            first, second = jnp.exp(log_p - top), jnp.exp(log_n - top)
            share_p = first / (first + second)
            share_n = second / ((first + second) * total_n)
            share_p = jnp.sum(jnp.where(eye, share_p, 0.0), axis=1, keepdims=True)
            share_n = jnp.sum(jnp.where(eye, share_n, 0.0), axis=1, keepdims=True)
            prompt = message[:TILE]
            newest = numer_ref[owner].astype(jnp.float32)
            merged = (prompt * share_p + newest * share_n)
            for j in range(HEADS):
                rows = merged[j * SLAB:(j + 1) * SLAB].reshape(PROMPT_SAMPLES, STEPS, HEAD_SIZE)
                samples = pl.ds(owner * PROMPT_SAMPLES, PROMPT_SAMPLES)
                out[samples, :, pl.ds(j * HEAD_SIZE, HEAD_SIZE)] = rows.astype(jnp.bfloat16)
        return carry

    lax.fori_loop(0, OWNERS // 16, some, 0)


def diagonal():
    first = lax.broadcasted_iota(jnp.int32, (TILE, HEAD_SIZE), 0)
    return first == lax.broadcasted_iota(jnp.int32, (TILE, HEAD_SIZE), 1)


VMEM = pl.BlockSpec(memory_space=pltpu.VMEM)
SMEM = pl.BlockSpec(memory_space=pltpu.SMEM)
ANY = pl.BlockSpec(memory_space=pl.ANY)


def params(mib):
    return pltpu.CompilerParams(vmem_limit_bytes=mib * MiB)


def body(
    new_states,
    w_query,
    keyvalue_weight,
    keyvalue_pages,
    page_table,
    prompt_pages,
    share_prompt,
    share_group,
):
    groups = lax.axis_size("dp")
    width = new_states.shape[2]
    tensor = lax.axis_index("tensor")
    place = jnp.stack([tensor // C, tensor % C]).astype(jnp.int32)

    targets = jnp.arange(groups, dtype=jnp.int32)
    match = (share_group[0][:, None] == targets[None, :]).astype(jnp.int32)
    dest_prompt = jnp.sum(match * share_prompt[0][:, None], axis=0)
    choose = (
        dest_prompt[:, None] == jnp.arange(prompt_pages.shape[1], dtype=jnp.int32)[None, :]
    ).astype(jnp.int32)
    dest_count = jnp.sum(choose * prompt_pages[0][None, :], axis=1)
    logical = (
        dest_prompt[:, None] * LONGEST_PAGES + jnp.arange(LONGEST_PAGES, dtype=jnp.int32)[None, :]
    )
    lookup = (
        logical[:, :, None] == jnp.arange(page_table.shape[1], dtype=jnp.int32)[None, None, :]
    ).astype(jnp.int32)
    physical = jnp.sum(lookup * page_table[0][None, None, :], axis=2).reshape(-1)
    slot_count = lax.all_to_all(dest_count, "dp", split_axis=0, concat_axis=0, tiled=True)
    cosine, sine = rope_tables()
    wkv = keyvalue_weight.reshape(width, -1)

    rows = new_states.shape[0] * STEPS
    own = pl.pallas_call(
        norm_kernel,
        out_shape=jax.ShapeDtypeStruct((rows, width), jnp.bfloat16),
        in_specs=[VMEM],
        out_specs=VMEM,
        scratch_shapes=[pltpu.VMEM((rows, width), jnp.float32)],
        compiler_params=params(8),
        name="norm",
    )(new_states)
    ahead = lax.ppermute(own, "tensor", along_x(1))
    behind = lax.ppermute(own, "tensor", along_x(-1))
    own_theirs = lax.ppermute(own, "tensor", other_core())

    def project_near(deltas, *slabs):
        return pl.pallas_call(
            functools.partial(near_kernel, deltas),
            out_shape=jax.ShapeDtypeStruct(
                (len(deltas), Z, TILE + 2 * SLAB, HEAD_SIZE), jnp.bfloat16
            ),
            in_specs=[SMEM] * 2 + [VMEM] * (len(slabs) + 4),
            out_specs=VMEM,
            compiler_params=params(16),
            name="project_near",
        )(place, slot_count, *slabs, w_query, wkv, cosine, sine)

    first = project_near((0,), own, own_theirs)
    half = jax.ShapeDtypeStruct((rows // 2, width), jnp.bfloat16)
    both, far_0, far_1 = pl.pallas_call(
        forward_kernel,
        out_shape=(jax.ShapeDtypeStruct((2 * rows, width), jnp.bfloat16), half, half),
        in_specs=[VMEM] * 3,
        out_specs=(VMEM,) * 3,
        compiler_params=params(4),
        name="forward",
    )(ahead, behind, first)
    far_0 = lax.ppermute(far_0, "tensor", along_x(1))
    far_1 = lax.ppermute(far_1, "tensor", along_x(-1))
    both_theirs = lax.ppermute(both, "tensor", other_core())
    near = project_near((1, 3), both, both_theirs)

    far = pl.pallas_call(
        join_kernel,
        out_shape=jax.ShapeDtypeStruct((rows, width), jnp.bfloat16),
        in_specs=[VMEM] * 3,
        out_specs=VMEM,
        compiler_params=params(4),
        name="join",
    )(far_0, far_1, near)
    far_theirs = lax.ppermute(far, "tensor", other_core())
    queries, keyvals = pl.pallas_call(
        far_kernel,
        out_shape=(
            jax.ShapeDtypeStruct((OWNERS, TILE, HEAD_SIZE), jnp.bfloat16),
            jax.ShapeDtypeStruct((OWNERS, 2 * SLAB, HEAD_SIZE), jnp.bfloat16),
        ),
        in_specs=[SMEM] * 2 + [VMEM] * 8,
        out_specs=(VMEM,) * 2,
        compiler_params=params(12),
        name="project_far",
    )(place, slot_count, far, far_theirs, w_query, wkv, cosine, sine, first, near)

    asked = lax.all_to_all(queries, "dp", split_axis=0, concat_axis=0, tiled=True)
    newest = pl.pallas_call(
        newest_kernel,
        out_shape=(
            jax.ShapeDtypeStruct((OWNERS, TILE, HEAD_SIZE), jnp.bfloat16),
            jax.ShapeDtypeStruct((OWNERS, 8, TILE), jnp.float32),
        ),
        in_specs=[VMEM] * 2,
        out_specs=(VMEM,) * 2,
        compiler_params=params(8),
        name="newest_tokens",
    )(queries, keyvals)
    answers = pl.pallas_call(
        prompt_kernel,
        out_shape=jax.ShapeDtypeStruct((OWNERS, TILE + STAT_ROWS, HEAD_SIZE), jnp.bfloat16),
        in_specs=[SMEM] * 2 + [VMEM] * 3,
        out_specs=VMEM,
        compiler_params=params(8),
        name="prompt_attention",
    )(physical, dest_count, asked, keyvalue_pages, newest[1])
    back = lax.all_to_all(answers, "dp", split_axis=0, concat_axis=0, tiled=True)
    return pl.pallas_call(
        merge_kernel,
        out_shape=jax.ShapeDtypeStruct(
            (groups * PROMPT_SAMPLES, STEPS, HEADS * HEAD_SIZE), jnp.bfloat16
        ),
        in_specs=[VMEM] * 3,
        out_specs=VMEM,
        compiler_params=params(8),
        name="merge",
    )(back, *newest)


def solution(mesh):
    placed = (
        P(("dp", "tensor"), None, None),
        P(None, "tensor"),
        P(None, "tensor", None),
        P("dp", "tensor", None, None),
        P("dp", None),
        P("dp", None),
        P("dp", None),
        P("dp", None),
    )
    return jax.shard_map(
        body, mesh=mesh, in_specs=placed, out_specs=P("dp", None, "tensor"), check_vma=False
    )
```
